32 devices in a mesh: inner: 16 (over z, y, core), outer: 2 (over x).
Axes of the slice: x: 2, y: 2, z: 4, core: 2. Of those that a mesh axis runs over, the one named last changes fastest.
Arguments:
- queries: bfloat16 [4096, 1024], P(('outer', 'inner')), may hold values from -8 to 8
- key_rows: bfloat16 [4096, 128], P(('outer', 'inner')), may hold values from -8 to 8
- value_rows: bfloat16 [4096, 128], P(('outer', 'inner')), may hold values from -6 to 6
- grad_output: bfloat16 [4096, 1024], P(('outer', 'inner')), may hold values from -6 to 6
- doc_blocks: int32 [32], replicated, may hold values from 0 to 3, never falling along the last dimension, each value on 1 to 16 neighbouring positions
Outputs:
- grad_queries: bfloat16 [4096, 1024], P(('outer', 'inner'))
- grad_keys: bfloat16 [4096, 128], P(('outer', 'inner'))
- grad_values: bfloat16 [4096, 128], P(('outer', 'inner'))
The draws below stay inside these ranges and needn't reach their ends.
All inputs are finite; a program needn't handle non-finite values.
Results may differ from the reference program's by a relative error of at most 0.019.
Values may be sent and summed in bfloat16 or wider, within the bound.
No kernel may reach another device: no remote copies, remote signals or barrier semaphores. Data moves between devices by JAX's collectives and lax.ppermute only.
A program may use at most 64 MiB of HBM per device.

```python
import math
import jax
import jax.numpy as jnp
import numpy as np
from jax import lax

DH = 128
HEADS = 8
BLK = 128
NBLK = 32
SEQ = 4096
DOCBLK = 16


def draw_queries(key, part):
    return jnp.clip(jax.random.normal(jax.random.fold_in(key, 5), (SEQ, HEADS * DH), jnp.float32), -4.0, 4.0).astype(jnp.bfloat16)


def draw_key_rows(key, part):
    return jnp.clip(jax.random.normal(jax.random.fold_in(key, 6), (SEQ, DH), jnp.float32), -4.0, 4.0).astype(jnp.bfloat16)


def levels(own_key, shape, split, low, largest):
    loudness = 1.0
    for position, shards_of in split:
        draws = jax.random.uniform(jax.random.fold_in(jax.random.fold_in(own_key, 6), position), (shards_of,), jnp.float32, low / len(split), largest / len(split))
        loudness = loudness * jnp.repeat(jnp.exp(draws), shape[position] // shards_of).reshape((-1,) + (1,) * (len(shape) - 1 - position))
    return loudness


def length_profile(number_of, total, reach, slope):
    weights = [(1 << 20) // math.isqrt(rank ** slope) + 1 for rank in range(2, number_of + 1)]
    rest, counts = total - reach - (number_of - 1), [1] * (number_of - 1)
    while rest > 0:
        candidates = [i for i in range(number_of - 1) if counts[i] < reach]
        whole, remaining = sum([weights[i] for i in candidates]), rest
        for i in candidates:
            addition = min(reach - counts[i], max(1, remaining * weights[i] // whole), rest)
            counts[i] = counts[i] + addition
            rest = rest - addition
    return np.array([reach] + counts)


def ragged(rng, count, total, reach, lean):
    if count == 2:
        one = jax.random.randint(rng, (), max(1, total - reach), min(reach, total - 1) + 1)
        return jnp.stack([one, total - one])
    lengths = jnp.asarray(length_profile(count, total, reach, lean), jnp.int32)
    couples = (count - 1) // 2
    giver, receiver = lengths[1:1 + 2 * couples:2], lengths[2:2 + 2 * couples:2]
    margin = jnp.minimum(giver - 1, reach - receiver)
    moved = jax.random.randint(jax.random.fold_in(rng, 1), (couples,), 0, 1 << 20) % (margin + 1)
    lengths = lengths.at[1:1 + 2 * couples:2].set(giver - moved).at[2:2 + 2 * couples:2].set(receiver + moved)
    return lengths[jax.random.permutation(jax.random.fold_in(rng, 2), count)]


def noise(key, shape, scale, limit, cuts=(), kind=jnp.bfloat16):
    entries = scale * jax.random.normal(key, shape, jnp.float32)
    if cuts:
        entries = entries * levels(key, shape, cuts, -0.22, 0.18)
    return jnp.clip(entries, -limit, limit).astype(kind)


def setup_inputs(seed: int = 0) -> dict:
    key_of = jax.random.split(jax.random.key(seed), 6)
    queries = draw_queries(jax.random.fold_in(key_of[5], 71), 0)
    key_rows = draw_key_rows(jax.random.fold_in(key_of[5], 71), 0)
    value_rows = noise(key_of[2], (SEQ, DH), 1.0, 6.0, ((0, 32),))
    grad_output = noise(key_of[3], (SEQ, HEADS * DH), 1.0, 6.0, ((0, 32),))
    doc_blocks = jnp.searchsorted(jnp.cumsum(ragged(key_of[4], NBLK // 8, NBLK, DOCBLK, 2)), jnp.arange(NBLK), side="right").astype(jnp.int32)
    return {"queries": queries, "key_rows": key_rows, "value_rows": value_rows, "grad_output": grad_output, "doc_blocks": doc_blocks}


def reference(queries, key_rows, value_rows, grad_output, doc_blocks):
    scaling = DH ** -0.5
    span = DOCBLK * BLK
    keys_pad = jnp.concatenate([jnp.zeros((span, DH), key_rows.dtype), key_rows], axis=0)
    values_pad = jnp.concatenate([jnp.zeros((span, DH), value_rows.dtype), value_rows], axis=0)
    docs_pad = jnp.concatenate([jnp.full((DOCBLK,), -1, jnp.int32), doc_blocks.astype(jnp.int32)])
    query_blocks = queries.reshape(NBLK, BLK, HEADS, DH)
    grad_blocks = grad_output.reshape(NBLK, BLK, HEADS, DH)
    key_pos = jnp.arange(span, dtype=jnp.int32)
    query_pos = span - BLK + jnp.arange(BLK, dtype=jnp.int32)

    def step(running, block_index):
        grad_k, grad_v = running
        first = ((block_index + 1) * BLK).astype(jnp.int32)
        key_win = lax.dynamic_slice_in_dim(keys_pad, first, span, 0).astype(jnp.float32)
        value_win = lax.dynamic_slice_in_dim(values_pad, first, span, 0).astype(jnp.float32)
        tags = lax.dynamic_slice_in_dim(docs_pad, (block_index + 1).astype(jnp.int32), DOCBLK, 0)
        key_tags = jnp.repeat(tags, BLK)
        own_tag = lax.dynamic_index_in_dim(doc_blocks, block_index, 0, keepdims=False)
        allowed = (key_tags[None, :] == own_tag) & (key_pos[None, :] <= query_pos[:, None])
        allowed = allowed[:, None, :]
        query_here = lax.dynamic_index_in_dim(query_blocks, block_index, 0, keepdims=False).astype(jnp.float32)
        grad_here = lax.dynamic_index_in_dim(grad_blocks, block_index, 0, keepdims=False).astype(jnp.float32)
        scores = jnp.einsum('thd,kd->thk', query_here, key_win) * scaling
        row_max = jnp.max(jnp.where(allowed, scores, -jnp.inf), axis=-1, keepdims=True)
        weights = jnp.exp(jnp.where(allowed, scores - row_max, -jnp.inf))
        row_sum = jnp.sum(weights, axis=-1, keepdims=True)
        probs = weights / row_sum
        attn_out = jnp.einsum('thk,kd->thd', probs, value_win, precision=lax.Precision.HIGHEST)
        delta = jnp.sum(grad_here * attn_out, axis=-1, keepdims=True)
        probs_low = probs.astype(jnp.bfloat16).astype(jnp.float32)
        value_part = jnp.einsum('thk,thd->kd', probs_low, grad_here)
        dprobs = jnp.einsum('thd,kd->thk', grad_here, value_win)
        dscores = (probs * (dprobs - delta) * scaling).astype(jnp.bfloat16).astype(jnp.float32)
        grad_q = jnp.einsum('thk,kd->thd', dscores, key_win).astype(jnp.bfloat16)
        key_part = jnp.einsum('thk,thd->kd', dscores, query_here)
        grad_k = lax.dynamic_update_slice_in_dim(grad_k, lax.dynamic_slice_in_dim(grad_k, first, span, 0) + key_part, first, 0)
        grad_v = lax.dynamic_update_slice_in_dim(grad_v, lax.dynamic_slice_in_dim(grad_v, first, span, 0) + value_part, first, 0)
        return (grad_k, grad_v), grad_q

    start_state = (jnp.zeros((SEQ + span, DH), jnp.float32), jnp.zeros((SEQ + span, DH), jnp.float32))
    (grad_k, grad_v), grad_q = lax.scan(step, start_state, jnp.arange(NBLK, dtype=jnp.int32))
    grad_queries = grad_q.reshape(SEQ, HEADS * DH)
    return grad_queries, grad_k[span:].astype(jnp.bfloat16), grad_v[span:].astype(jnp.bfloat16)
```

```python
import functools
import math

import jax
import jax.numpy as jnp
from jax import lax
from jax.experimental import pallas as pl
from jax.experimental.pallas import tpu as pltpu
from jax.sharding import PartitionSpec as P

BLOCKED = -1e30


def window_ids(at, span):
    half = span // 2

    def earlier(t, bit):
        upper = (t // bit) % 2
        return [t - span * upper] + received(t, bit)

    def received(t, bit):
        pieces = [t - half]
        step = half // 2
        while step > bit:
            partner = t + step - 2 * step * ((t // step) % 2)
            pieces = pieces + earlier(partner, step)
            step //= 2
        return pieces

    return [at] + received(at, 0) if span > 1 else [at]


def attention_kernel(span, width, block_len, doc_ref, at_ref, q_ref, g_ref, kv_ref, dq_ref, dkv_ref, kt_ref, s_ref, dp_ref, dk_ref, dv_ref):
    at = at_ref[0]
    keys = span * block_len
    scale = width ** -0.5
    scale2 = scale * math.log2(math.e)
    ids = window_ids(at, span)
    own_doc = doc_ref[at]
    bias = [
        jnp.where((one >= 0) & (doc_ref[jnp.maximum(one, 0)] == own_doc), 0.0, BLOCKED).astype(jnp.float32)
        for one in ids
    ]
    heads = q_ref.shape[1] // width
    pair = 2 * block_len
    per_chunk = 4
    chunks = [(c, min(per_chunk, span - c)) for c in range(0, span, per_chunk)]
    kt_ref[...] = kv_ref[:, :width].T
    key_pos = lax.broadcasted_iota(jnp.int32, (block_len, pair), 0)
    row_pos = lax.broadcasted_iota(jnp.int32, (block_len, pair), 1) % block_len
    causal = key_pos <= row_pos
    nt = (((1,), (1,)), ((), ()))

    def fold(tile, op):
        return op(tile.reshape(-1, 8, pair), axis=0)

    for hp in range(heads // 2):
        left = 2 * hp * width
        q_rows = jnp.concatenate([q_ref[:, left : left + width], q_ref[:, left + width : left + 2 * width]], axis=0)
        g_rows = jnp.concatenate([g_ref[:, left : left + width], g_ref[:, left + width : left + 2 * width]], axis=0)
        top = None
        for first, count in chunks:
            rows = slice(first * block_len, (first + count) * block_len)
            s = lax.dot_general(kv_ref[rows, :width], q_rows, nt, preferred_element_type=jnp.float32)
            for i in range(count):
                part = s[i * block_len : (i + 1) * block_len]
                if first + i == 0:
                    part = jnp.where(causal, part, BLOCKED)
                s_ref[(first + i) * block_len : (first + i + 1) * block_len, :] = part
                best = fold(part, jnp.max) + bias[first + i]
                top = best if top is None else jnp.maximum(top, best)
        top = jnp.max(top, axis=0, keepdims=True) * scale2
        total = jnp.zeros((8, pair), jnp.float32)
        inner = jnp.zeros((8, pair), jnp.float32)
        for first, count in chunks:
            rows = slice(first * block_len, (first + count) * block_len)
            dp = lax.dot_general(kv_ref[rows, width:], g_rows, nt, preferred_element_type=jnp.float32)
            for i in range(count):
                at_rows = slice((first + i) * block_len, (first + i + 1) * block_len)
                dp_part = dp[i * block_len : (i + 1) * block_len]
                p = jnp.exp2(s_ref[at_rows, :] * scale2 + (bias[first + i] - top))
                s_ref[at_rows, :] = p
                dp_ref[at_rows, :] = dp_part
                total = total + fold(p, jnp.sum)
                inner = inner + fold(p * dp_part, jnp.sum)
        total = jnp.sum(total, axis=0, keepdims=True)
        inverse = 1.0 / total
        delta = jnp.sum(inner, axis=0, keepdims=True) * inverse
        scaled = inverse * scale
        dq = None
        for first, count in chunks:
            rows = slice(first * block_len, (first + count) * block_len)
            p = s_ref[rows, :]
            low = (p * inverse).astype(jnp.bfloat16)
            ds = ((p * scaled) * (dp_ref[rows, :] - delta)).astype(jnp.bfloat16)
            dv = jnp.dot(low, g_rows, preferred_element_type=jnp.float32)
            dk = jnp.dot(ds, q_rows, preferred_element_type=jnp.float32)
            part = jnp.dot(kt_ref[:, rows], ds, preferred_element_type=jnp.float32)
            dq = part if dq is None else dq + part
            if hp > 0:
                dk = dk_ref[rows, :] + dk
                dv = dv_ref[rows, :] + dv
            if hp < heads // 2 - 1:
                dk_ref[rows, :] = dk
                dv_ref[rows, :] = dv
            else:
                dkv_ref[rows, :width] = dk.astype(jnp.bfloat16)
                dkv_ref[rows, width:] = dv.astype(jnp.bfloat16)
        for h in range(2):
            dq_ref[:, left + h * width : left + (h + 1) * width] = dq[:, h * block_len : (h + 1) * block_len].T.astype(jnp.bfloat16)


def attention(span, doc_blocks, at, queries, grad_output, kv):
    block_len, columns = queries.shape
    width = kv.shape[1] // 2
    keys = span * block_len
    vmem = pl.BlockSpec(memory_space=pltpu.VMEM)
    smem = pl.BlockSpec(memory_space=pltpu.SMEM)
    rows = columns // width * block_len
    return pl.pallas_call(
        functools.partial(attention_kernel, span, width, block_len),
        out_shape=(
            jax.ShapeDtypeStruct(queries.shape, jnp.bfloat16),
            jax.ShapeDtypeStruct((keys, 2 * width), jnp.bfloat16),
        ),
        in_specs=[smem, smem, vmem, vmem, vmem],
        out_specs=(vmem, vmem),
        scratch_shapes=[
            pltpu.VMEM((width, keys), jnp.bfloat16),
            pltpu.VMEM((keys, 2 * block_len), jnp.float32),
            pltpu.VMEM((keys, 2 * block_len), jnp.float32),
            pltpu.VMEM((keys, width), jnp.float32),
            pltpu.VMEM((keys, width), jnp.float32),
        ],
        compiler_params=pltpu.CompilerParams(vmem_limit_bytes=40 * 1024 * 1024),
        cost_estimate=pl.CostEstimate(
            flops=10 * keys * rows * width,
            bytes_accessed=6 * rows * width + 6 * keys * width * 2,
            transcendentals=keys * rows,
        ),
        name="attention",
    )(doc_blocks, at, queries, grad_output, kv)


def shards(inner_count, outer_count, queries, key_rows, value_rows, grad_output, doc_blocks):
    width = key_rows.shape[1]
    block_len = key_rows.shape[0]
    span = inner_count
    half = span // 2
    devices = inner_count * outer_count
    inner_at = lax.axis_index("inner")
    outer_at = lax.axis_index("outer")
    at = outer_at * inner_count + inner_at

    def place(t):
        return (t % inner_count) * outer_count + t // inner_count

    def moved(x, distance):
        route = [(place(t), place((t + distance) % devices)) for t in range(devices)]
        return lax.ppermute(x, ("inner", "outer"), route)

    def grouped(x, distance):
        return lax.ppermute(x, "outer", [(i, (i + distance) % outer_count) for i in range(outer_count)])

    def swapped(x, bit):
        return lax.ppermute(x, "inner", [(i, i ^ bit) for i in range(inner_count)])

    def upper(bit):
        return (inner_at // bit) % 2 == 1

    own = jnp.concatenate([key_rows, value_rows], axis=1)
    held = moved(own, half)
    prior = grouped(own, 1)
    bits = []
    bit = half // 2
    while bit >= 1:
        bits.append(bit)
        bit //= 2
    for bit in bits:
        first = jnp.where(upper(bit), prior, own)
        held = jnp.concatenate([held, swapped(jnp.concatenate([first, held], axis=0), bit)], axis=0)
    window = jnp.concatenate([own, held], axis=0)

    grad_queries, parts = attention(span, doc_blocks, at.reshape(1), queries, grad_output, window)

    mine = parts[:block_len].astype(jnp.float32)
    before = jnp.zeros_like(mine)
    held = parts[block_len:]
    for bit in reversed(bits):
        kept = held.shape[0] // 2 if False else (half // bit - 1) * block_len
        got = swapped(held[kept:], bit)
        first = got[:block_len].astype(jnp.float32)
        mine = mine + jnp.where(upper(bit), 0.0, first)
        before = before + jnp.where(upper(bit), first, 0.0)
        held = (held[:kept].astype(jnp.float32) + got[block_len:].astype(jnp.float32)).astype(jnp.bfloat16)
    mine = mine + moved(held, -half).astype(jnp.float32) + grouped(before.astype(jnp.bfloat16), -1).astype(jnp.float32)
    grads = mine.astype(jnp.bfloat16)
    return grad_queries, grads[:, :width], grads[:, width:]


def solution(mesh):
    rows = P(("outer", "inner"), None)
    body = functools.partial(shards, mesh.shape["inner"], mesh.shape["outer"])
    return jax.shard_map(
        body, mesh=mesh, in_specs=(rows, rows, rows, rows, P()), out_specs=(rows, rows, rows), check_vma=False
    )
```

```python
import functools
import math

import jax
import jax.numpy as jnp
from jax import lax
from jax.experimental import pallas as pl
from jax.experimental.pallas import tpu as pltpu
from jax.sharding import PartitionSpec as P

BLOCKED = -1e30
F32 = jnp.float32
LOW = jnp.bfloat16


def strides(span):
    return list(range(2, span // 2, 2))


def window_ids(at, span):
    def nearest(t, u):
        return jnp.where(u < t, u, u - span)

    def same_core(t):
        others = [t ^ d for d in strides(span)]
        return [nearest(t, u) for u in others], [u - span // 2 for u in others]

    near, far = same_core(at)
    twin = at ^ 1
    twin_near, twin_far = same_core(twin)
    return [at, at - span // 2] + near + far + [nearest(at, twin), twin - span // 2] + twin_near + twin_far


def attention_kernel(span, width, block_len, doc_ref, at_ref, q_ref, g_ref, kv_ref, dq_ref, own_ref, far_ref, nears_ref, fars_ref, twin_near_ref, twin_far_ref, kt_ref, vt_ref, s_ref, p_ref, dk_ref, dv_ref):
    at = at_ref[0]
    keys = span * block_len
    scale = width**-0.5
    scale2 = scale * math.log2(math.e)
    own_doc = doc_ref[at]
    bias = [
        jnp.where((one >= 0) & (doc_ref[jnp.maximum(one, 0)] == own_doc), 0.0, BLOCKED).astype(F32)
        for one in window_ids(at, span)
    ]
    pairs = q_ref.shape[1] // width // 2
    pair = 2 * block_len
    steps = len(strides(span))
    twin = 2 + 2 * steps
    homes = [(own_ref, 0), (far_ref, 0)]
    homes += [(nears_ref, i) for i in range(steps)] + [(fars_ref, i) for i in range(steps)]
    homes += [(twin_near_ref, steps), (twin_far_ref, steps)]
    homes += [(twin_near_ref, i) for i in range(steps)] + [(twin_far_ref, i) for i in range(steps)]
    chunks = [(0, twin), (twin, span - twin)]
    kt_ref[...] = kv_ref[:, :width].T
    vt_ref[:width, :] = kv_ref[:, width:].T
    vt_ref[width:, :] = jnp.ones((vt_ref.shape[0] - width, keys), LOW)
    key_pos = lax.broadcasted_iota(jnp.int32, (block_len, pair), 0)
    row_pos = lax.broadcasted_iota(jnp.int32, (block_len, pair), 1) % block_len
    causal = key_pos <= row_pos
    nt = (((1,), (1,)), ((), ()))
    qt, gt, top, sums, state = ({} for _ in range(5))

    def slot(i):
        return slice(i * block_len, (i + 1) * block_len)

    def turned(ref, hp):
        left = 2 * hp * width
        return jnp.concatenate([ref[:, left : left + width].T, ref[:, left + width : left + 2 * width].T], axis=1)

    def score(hp, chunk):
        first, count = chunk
        rows = slice(first * block_len, (first + count) * block_len)
        s = jnp.dot(kv_ref[rows, :width], qt[hp], preferred_element_type=F32)
        for i in range(count):
            part = s[slot(i)]
            if first + i == 0:
                part = jnp.where(causal, part, BLOCKED)
            s_ref[hp % 2, slot(first + i), :] = part
            best = jnp.max(part.reshape(-1, 8, pair), axis=0) + bias[first + i]
            top[hp] = jnp.maximum(top[hp], best) if hp in top else best

    def weigh(hp, chunk):
        first, count = chunk
        for i in range(first, first + count):
            weights = jnp.exp2(s_ref[hp % 2, slot(i), :] * scale2 + (bias[i] - top[hp]))
            p_ref[hp % 2, slot(i), :] = weights.astype(LOW)
        rows = slice(first * block_len, (first + count) * block_len)
        part = jnp.dot(vt_ref[:, rows], p_ref[hp % 2, rows, :], preferred_element_type=F32)
        sums[hp] = sums[hp] + part if hp in sums else part

    def settle(hp):
        inverse = 1.0 / sums[hp][width : width + 1]
        wide_g = gt[hp].astype(F32)
        delta = jnp.sum(sums[hp][:width] * wide_g, axis=0, keepdims=True) * inverse
        scaled_q = (qt[hp].astype(F32) * (inverse * scale)).astype(LOW)
        scaled_g = (wide_g * inverse).astype(LOW)
        state[hp] = [inverse * scale, delta, scaled_q, scaled_g, None]

    def spread(hp, chunk):
        unused_factor, delta, scaled_q, scaled_g, dq = state[hp]
        first, count = chunk
        rows = slice(first * block_len, (first + count) * block_len)
        dp = jnp.dot(kv_ref[rows, width:], gt[hp], preferred_element_type=F32)
        low = p_ref[hp % 2, rows, :]
        ds = (low.astype(F32) * (dp - delta)).astype(LOW)
        dv = lax.dot_general(low, scaled_g, nt, preferred_element_type=F32)
        dk = lax.dot_general(ds, scaled_q, nt, preferred_element_type=F32)
        part = jnp.dot(kt_ref[:, rows], ds, preferred_element_type=F32)
        state[hp][4] = part if dq is None else dq + part
        if hp > 0:
            dk = dk_ref[rows, :] + dk
            dv = dv_ref[rows, :] + dv
        if hp < pairs - 1:
            dk_ref[rows, :] = dk
            dv_ref[rows, :] = dv
            return
        dk, dv = dk.astype(LOW), dv.astype(LOW)
        for i in range(count):
            home, place = homes[first + i]
            home[slot(place), :width] = dk[slot(i)]
            home[slot(place), width:] = dv[slot(i)]

    def finish(hp):
        left = 2 * hp * width
        dq = state[hp][4] * state[hp][0]
        for h in range(2):
            dq_ref[:, left + h * width : left + (h + 1) * width] = dq[:, slot(h)].T.astype(LOW)

    def load(hp):
        qt[hp], gt[hp] = turned(q_ref, hp), turned(g_ref, hp)

    def peak(hp):
        top[hp] = jnp.max(top[hp], axis=0, keepdims=True) * scale2

    for hp in range(-2, pairs):
        if hp >= 0:
            settle(hp)
        if 0 <= hp + 1 < pairs:
            peak(hp + 1)
        if hp + 2 < pairs:
            load(hp + 2)
        for chunk in chunks:
            if 0 <= hp + 1 < pairs:
                weigh(hp + 1, chunk)
            if hp + 2 < pairs:
                score(hp + 2, chunk)
            if hp >= 0:
                spread(hp, chunk)
        if hp >= 0:
            finish(hp)


def attention(span, doc_blocks, at, queries, grad_output, kv):
    block_len, columns = queries.shape
    width = kv.shape[1] // 2
    keys = span * block_len
    rows = columns // width * block_len
    steps = len(strides(span))
    vmem = pl.BlockSpec(memory_space=pltpu.VMEM)
    smem = pl.BlockSpec(memory_space=pltpu.SMEM)
    slots = [1, 1, steps, steps, steps + 1, steps + 1]
    return pl.pallas_call(
        functools.partial(attention_kernel, span, width, block_len),
        out_shape=(
            jax.ShapeDtypeStruct(queries.shape, LOW),
            *(jax.ShapeDtypeStruct((n * block_len, 2 * width), LOW) for n in slots),
        ),
        in_specs=[smem, smem, vmem, vmem, vmem],
        out_specs=(vmem,) * 7,
        scratch_shapes=[
            pltpu.VMEM((width, keys), LOW),
            pltpu.VMEM((width + 16, keys), LOW),
            pltpu.VMEM((2, keys, 2 * block_len), F32),
            pltpu.VMEM((2, keys, 2 * block_len), LOW),
            pltpu.VMEM((keys, width), F32),
            pltpu.VMEM((keys, width), F32),
        ],
        compiler_params=pltpu.CompilerParams(vmem_limit_bytes=40 * 1024 * 1024),
        cost_estimate=pl.CostEstimate(
            flops=12 * keys * rows * width,
            bytes_accessed=6 * rows * width + 6 * keys * width * 2,
            transcendentals=keys * rows,
        ),
        name="attention",
    )(doc_blocks, at, queries, grad_output, kv)


def shards(inner_count, outer_count, queries, key_rows, value_rows, grad_output, doc_blocks):
    width = key_rows.shape[1]
    block_len = key_rows.shape[0]
    span = inner_count
    half = span // 2
    devices = inner_count * outer_count
    inner_at = lax.axis_index("inner")
    outer_at = lax.axis_index("outer")
    at = outer_at * inner_count + inner_at
    ways = strides(span)

    def place(t):
        return (t % inner_count) * outer_count + t // inner_count

    def moved(x, distance):
        route = [(place(t), place((t + distance) % devices)) for t in range(devices)]
        return lax.ppermute(x, ("inner", "outer"), route)

    def grouped(x, distance):
        return lax.ppermute(x, "outer", [(i, (i + distance) % outer_count) for i in range(outer_count)])

    def swapped(x, d):
        return lax.ppermute(x, "inner", [(i, i ^ d) for i in range(inner_count)])

    def above(d):
        return inner_at > (inner_at ^ d)

    def block(x, i):
        return x[i * block_len : (i + 1) * block_len]

    own = jnp.concatenate([key_rows, value_rows], axis=1)
    prior = grouped(own, 1)
    far = moved(own, half)
    nears = [swapped(jnp.where(above(d), prior, own), d) for d in ways]
    fars = [swapped(far, d) for d in ways]
    nears, fars = jnp.concatenate(nears, axis=0), jnp.concatenate(fars, axis=0)
    twin_first = swapped(jnp.concatenate([jnp.where(above(1), prior, own), far], axis=0), 1)
    twin_nears, twin_fars = swapped(nears, 1), swapped(fars, 1)
    window = jnp.concatenate([own, far, nears, fars, twin_first, twin_nears, twin_fars], axis=0)

    grad_queries, own_part, far_part, near_parts, far_parts, twin_near, twin_far = attention(
        span, doc_blocks, at.reshape(1), queries, grad_output, window
    )

    def added(x, y):
        return (x.astype(F32) + y.astype(F32)).astype(LOW)

    steps = len(ways)
    from_twin_far = swapped(twin_far, 1)
    from_twin_near = swapped(twin_near, 1)
    far_back = [swapped(added(block(far_parts, i), block(from_twin_far, i)), d) for i, d in enumerate(ways)]
    near_back = [swapped(added(block(near_parts, i), block(from_twin_near, i)), d) for i, d in enumerate(ways)]
    far_sum = far_part.astype(F32) + block(from_twin_far, steps).astype(F32)
    for one in far_back:
        far_sum = far_sum + one.astype(F32)
    far_home = moved(far_sum.astype(LOW), -half)
    mine = own_part.astype(F32)
    before = jnp.zeros_like(mine)
    for d, one in zip([1] + ways, [block(from_twin_near, steps)] + near_back):
        one = one.astype(F32)
        mine = mine + jnp.where(above(d), 0.0, one)
        before = before + jnp.where(above(d), one, 0.0)
    prior_home = grouped(before.astype(LOW), -1)
    grads = (mine + far_home.astype(F32) + prior_home.astype(F32)).astype(LOW)
    return grad_queries, grads[:, :width], grads[:, width:]


def solution(mesh):
    rows = P(("outer", "inner"), None)
    body = functools.partial(shards, mesh.shape["inner"], mesh.shape["outer"])
    return jax.shard_map(
        body, mesh=mesh, in_specs=(rows, rows, rows, rows, P()), out_specs=(rows, rows, rows), check_vma=False
    )
```

```python
import functools
import math

import jax
import jax.numpy as jnp
from jax import lax
from jax.experimental import pallas as pl
from jax.experimental.pallas import tpu as pltpu
from jax.sharding import PartitionSpec as P

BLOCKED = -1e30
F32 = jnp.float32
LOW = jnp.bfloat16


def strides(span):
    return list(range(span // 2 - 2, 0, -2))


def window_ids(at, span):
    def nearest(t, u):
        return jnp.where(u < t, u, u - span)

    def same_core(t):
        others = [t ^ d for d in strides(span)]
        return [nearest(t, u) for u in others], [u - span // 2 for u in others]

    near, far = same_core(at)
    twin = at ^ 1
    twin_near, twin_far = same_core(twin)
    early = [at, at - span // 2] + near + [nearest(at, twin), twin - span // 2]
    return early, far + twin_near + twin_far


def biases(doc_ref, at, ids):
    own_doc = doc_ref[at]
    return [
        jnp.where((one >= 0) & (doc_ref[jnp.maximum(one, 0)] == own_doc), 0.0, BLOCKED).astype(F32) for one in ids
    ]


def peaks(tile, bias):
    return jnp.max(tile.reshape(-1, 8, tile.shape[1]), axis=0) + bias


def pack_kernel(k_hbm, v_hbm, kv_ref, arrived):
    width = k_hbm.shape[1]
    copies = [
        pltpu.make_async_copy(one, kv_ref.at[:, pl.ds(i * width, width)], arrived.at[i])
        for i, one in enumerate((k_hbm, v_hbm))
    ]
    for copy in copies:
        copy.start()
    for copy in copies:
        copy.wait()


def early_kernel(span, width, block_len, doc_hbm, at_ref, q_hbm, g_hbm, kv_ref, qt_ref, gt_ref, vt_ref, s_ref, dp_ref, top_ref, bias_ref, q_ref, g_ref, doc_ref, arrived):
    places = enumerate(((q_hbm, q_ref), (g_hbm, g_ref), (doc_hbm, doc_ref)))
    copies = [pltpu.make_async_copy(there, here, arrived.at[i]) for i, (there, here) in places]
    for copy in copies:
        copy.start()
    pair = 2 * block_len
    vt_ref[:width, :] = kv_ref[:, width:].T
    vt_ref[width:, :] = jnp.ones((vt_ref.shape[0] - width, vt_ref.shape[1]), LOW)
    key_pos = lax.broadcasted_iota(jnp.int32, (block_len, pair), 0)
    row_pos = lax.broadcasted_iota(jnp.int32, (block_len, pair), 1) % block_len
    causal = key_pos <= row_pos
    for copy in copies:
        copy.wait()
    at = at_ref[0]
    early_ids, late_ids = window_ids(at, span)
    bias = biases(doc_ref, at, early_ids + late_ids)
    for i, one in enumerate(bias):
        bias_ref[8 * i : 8 * i + 8, :] = jnp.full((8, pair), one)
    for hp in range(q_ref.shape[1] // width // 2):
        left = 2 * hp * width
        lanes = slice(hp * pair, (hp + 1) * pair)
        for h in range(2):
            head = slice(left + h * width, left + (h + 1) * width)
            place = slice(hp * pair + h * block_len, hp * pair + (h + 1) * block_len)
            qt_ref[:, place] = q_ref[:, head].T
            gt_ref[:, place] = g_ref[:, head].T
        s = jnp.dot(kv_ref[:, :width], qt_ref[:, lanes], preferred_element_type=F32)
        dp_ref[:, lanes] = jnp.dot(kv_ref[:, width:], gt_ref[:, lanes], preferred_element_type=F32)
        top = None
        for i, one in enumerate(bias[: len(early_ids)]):
            slot = slice(i * block_len, (i + 1) * block_len)
            part = s[slot]
            if i == 0:
                part = jnp.where(causal, part, BLOCKED)
            s_ref[slot, lanes] = part
            best = peaks(part, one)
            top = best if top is None else jnp.maximum(top, best)
        top_ref[:, lanes] = top


def main_kernel(span, width, block_len, bias_ref, qt_ref, gt_ref, vte_ref, se_ref, dpe_ref, tope_ref, kv_ref, first_ref, twin_near_ref, twin_far_ref, p_ref, ds_ref, sq_ref, sg_ref, factor_ref, vt_ref, s_ref, dk_ref, dv_ref):
    scale = width**-0.5
    scale2 = scale * math.log2(math.e)
    pairs = qt_ref.shape[1] // block_len // 2
    pair = 2 * block_len
    steps = len(strides(span))
    early = steps + 4
    vt_ref[:width, :] = kv_ref[:, width:].T
    vt_ref[width:, :] = jnp.ones((vt_ref.shape[0] - width, vt_ref.shape[1]), LOW)
    nt = (((1,), (1,)), ((), ()))
    homes = [(first_ref, 0), (twin_far_ref, steps)]
    homes += [(twin_near_ref, i) for i in range(steps)] + [(twin_far_ref, i) for i in range(steps)]
    twin_slots = {0: (early - 2, 2, 0), 1: (early + steps, 2 * steps, 2)}
    spans = {0: (0, early), 1: (early, span)}
    top, sums, state = {}, {}, {}

    def rows_of(first, end):
        return slice(first * block_len, end * block_len)

    def lanes_of(hp):
        return slice(hp * pair, (hp + 1) * pair)

    def score(hp):
        s = jnp.dot(kv_ref[:, :width], qt_ref[:, lanes_of(hp)], preferred_element_type=F32)
        s_ref[hp % 2, :, :] = s
        top[hp] = tope_ref[:, lanes_of(hp)]
        for i in range(early, span):
            top[hp] = jnp.maximum(top[hp], peaks(s[rows_of(i - early, i - early + 1)], bias_ref[8 * i : 8 * i + 8, :]))

    def peak(hp):
        top[hp] = jnp.max(top[hp], axis=0, keepdims=True) * scale2

    def weigh(hp, part):
        first, end = spans[part]
        for i in range(first, end):
            s = s_ref[hp % 2, rows_of(i - early, i - early + 1), :] if part else se_ref[rows_of(i, i + 1), lanes_of(hp)]
            p_ref[rows_of(i, i + 1), lanes_of(hp)] = jnp.exp2(s * scale2 + (bias_ref[8 * i : 8 * i + 1, :] - top[hp])).astype(LOW)
        turned = vt_ref if part else vte_ref
        more = jnp.dot(turned[...], p_ref[rows_of(first, end), lanes_of(hp)], preferred_element_type=F32)
        sums[hp] = sums[hp] + more if hp in sums else more

    def settle(hp):
        inverse = 1.0 / sums[hp][width : width + 1]
        wide_g = gt_ref[:, lanes_of(hp)].astype(F32)
        delta = jnp.sum(sums[hp][:width] * wide_g, axis=0, keepdims=True) * inverse
        scaled_q = (qt_ref[:, lanes_of(hp)].astype(F32) * (inverse * scale)).astype(LOW)
        scaled_g = (wide_g * inverse).astype(LOW)
        sq_ref[:, lanes_of(hp)] = scaled_q
        sg_ref[:, lanes_of(hp)] = scaled_g
        factor_ref[:, lanes_of(hp)] = jnp.broadcast_to(inverse * scale, (8, pair))
        state[hp] = (delta, scaled_q, scaled_g)

    def spread(hp, part):
        delta, scaled_q, scaled_g = state[hp]
        first, end = spans[part]
        rows = rows_of(first, end)
        if part:
            dp = jnp.dot(kv_ref[:, width:], gt_ref[:, lanes_of(hp)], preferred_element_type=F32)
        else:
            dp = dpe_ref[:, lanes_of(hp)]
        ds_ref[rows, lanes_of(hp)] = (p_ref[rows, lanes_of(hp)].astype(F32) * (dp - delta)).astype(LOW)
        at_slot, count, place = twin_slots[part]
        rows, kept = rows_of(at_slot, at_slot + count), rows_of(place, place + count)
        dv = lax.dot_general(p_ref[rows, lanes_of(hp)], scaled_g, nt, preferred_element_type=F32)
        dk = lax.dot_general(ds_ref[rows, lanes_of(hp)], scaled_q, nt, preferred_element_type=F32)
        if hp > 0:
            dk = dk_ref[kept, :] + dk
            dv = dv_ref[kept, :] + dv
        if hp < pairs - 1:
            dk_ref[kept, :] = dk
            dv_ref[kept, :] = dv
            return
        dk, dv = dk.astype(LOW), dv.astype(LOW)
        for i in range(count):
            home, where = homes[place + i]
            home[rows_of(where, where + 1), :width] = dk[rows_of(i, i + 1)]
            home[rows_of(where, where + 1), width:] = dv[rows_of(i, i + 1)]

    for hp in range(-2, pairs):
        if hp >= 0:
            settle(hp)
        if 0 <= hp + 1 < pairs:
            peak(hp + 1)
        for part in (0, 1):
            if 0 <= hp + 1 < pairs:
                weigh(hp + 1, part)
            if hp + 2 < pairs and part == 0:
                score(hp + 2)
            if hp >= 0:
                spread(hp, part)


def kept_kernel(span, width, block_len, p_ref, ds_ref, sq_ref, sg_ref, own_ref, far_ref, nears_ref, fars_ref):
    steps = len(strides(span))
    nt = (((1,), (1,)), ((), ()))
    for slot, refs in ((0, (own_ref, far_ref, nears_ref)), (4 + steps, (fars_ref,))):
        count = sum(ref.shape[0] for ref in refs)
        rows = slice(slot * block_len, slot * block_len + count)
        dk = lax.dot_general(ds_ref[rows, :], sq_ref[...], nt, preferred_element_type=F32).astype(LOW)
        dv = lax.dot_general(p_ref[rows, :], sg_ref[...], nt, preferred_element_type=F32).astype(LOW)
        first = 0
        for ref in refs:
            ref[:, :width] = dk[first : first + ref.shape[0]]
            ref[:, width:] = dv[first : first + ref.shape[0]]
            first += ref.shape[0]


def query_kernel(width, block_len, unused_ref, ds_ref, factor_ref, early_ref, late_ref, dq_ref):
    early = early_ref.shape[0]
    early_t, late_t = early_ref[:, :width].T, late_ref[:, :width].T
    pair = 2 * block_len
    for hp in range(dq_ref.shape[1] // width // 2):
        lanes = slice(hp * pair, (hp + 1) * pair)
        dq = jnp.dot(early_t, ds_ref[:early, lanes], preferred_element_type=F32)
        dq = dq + jnp.dot(late_t, ds_ref[early:, lanes], preferred_element_type=F32)
        dq = dq * factor_ref[0:1, lanes]
        for h in range(2):
            head = slice((2 * hp + h) * width, (2 * hp + h + 1) * width)
            dq_ref[:, head] = dq[:, h * block_len : (h + 1) * block_len].T.astype(LOW)


HBM = pl.BlockSpec(memory_space=pltpu.HBM)
VMEM = pl.BlockSpec(memory_space=pltpu.VMEM)
SMEM = pl.BlockSpec(memory_space=pltpu.SMEM)


def in_hbm(x):
    return pltpu.with_memory_space_constraint(x, pltpu.HBM)


def call(body, name, ins, outs, scratch, flops, *operands):
    return pl.pallas_call(
        body,
        out_shape=tuple(jax.ShapeDtypeStruct(shape, kind) for shape, kind in outs),
        in_specs=ins,
        out_specs=(VMEM,) * len(outs),
        scratch_shapes=scratch,
        compiler_params=pltpu.CompilerParams(vmem_limit_bytes=24 * 1024 * 1024),
        cost_estimate=pl.CostEstimate(flops=flops, bytes_accessed=1 << 16, transcendentals=0),
        name=name,
    )(*operands)


def shards(inner_count, outer_count, queries, key_rows, value_rows, grad_output, doc_blocks):
    width = key_rows.shape[1]
    block_len = key_rows.shape[0]
    span = inner_count
    half = span // 2
    devices = inner_count * outer_count
    inner_at = lax.axis_index("inner")
    outer_at = lax.axis_index("outer")
    at = outer_at * inner_count + inner_at
    ways = strides(span)

    def place(t):
        return (t % inner_count) * outer_count + t // inner_count

    def moved(x, distance):
        route = [(place(t), place((t + distance) % devices)) for t in range(devices)]
        return lax.ppermute(x, ("inner", "outer"), route)

    def grouped(x, distance):
        return lax.ppermute(x, "outer", [(i, (i + distance) % outer_count) for i in range(outer_count)])

    def returned(x, d):
        route = []
        for t in range(devices):
            u = t ^ d
            route.append((place(t), place(u if u < t else (u - inner_count) % devices)))
        return lax.ppermute(x, ("inner", "outer"), route)

    def swapped(x, d):
        return lax.ppermute(x, "inner", [(i, i ^ d) for i in range(inner_count)])

    def above(d):
        return inner_at > (inner_at ^ d)

    def block(x, i):
        return x[i * block_len : (i + 1) * block_len]

    (own,) = call(
        pack_kernel,
        "pack",
        [HBM, HBM],
        [((block_len, 2 * width), LOW)],
        [pltpu.SemaphoreType.DMA((2,))],
        0,
        *(in_hbm(key_rows), in_hbm(value_rows)),
    )
    prior = grouped(own, 1)
    far = moved(own, half)
    nears = [swapped(jnp.where(above(d), prior, own), d) for d in ways]
    fars = [swapped(far, d) for d in ways[:-1]]
    nears, later_far = lax.optimization_barrier((jnp.concatenate(nears, axis=0), far))
    fars = jnp.concatenate(fars + [swapped(later_far, ways[-1])], axis=0)
    twin_first = swapped(jnp.concatenate([jnp.where(above(1), prior, own), far], axis=0), 1)
    twin_nears = swapped(nears, 1)
    early = jnp.concatenate([own, far, nears, twin_first], axis=0)

    steps = len(ways)
    heads = queries.shape[1] // width
    rows, keys = heads * block_len, span * block_len
    pair = 2 * block_len
    work = 2 * rows * width * block_len
    place_here = at.reshape(1)
    here = early.shape[0]
    turned = ((width, rows), LOW)

    def parts(n):
        return ((n * block_len, 2 * width), LOW)

    qt, gt, early_vt, early_s, early_dp, early_top, bias = call(
        functools.partial(early_kernel, span, width, block_len),
        "early",
        [HBM, SMEM, HBM, HBM, VMEM],
        [
            *(turned, turned, ((width + 16, here), LOW), ((here, rows), F32), ((here, rows), F32), ((8, rows), F32)),
            ((8 * span, pair), F32),
        ],
        [
            pltpu.VMEM(queries.shape, LOW),
            pltpu.VMEM(queries.shape, LOW),
            pltpu.SMEM(doc_blocks.shape, jnp.int32),
            pltpu.SemaphoreType.DMA((3,)),
        ],
        40 * work * (here // block_len),
        *(in_hbm(doc_blocks), place_here, in_hbm(queries), in_hbm(grad_output), early),
    )
    late = jnp.concatenate([fars, twin_nears, swapped(fars, 1)], axis=0)
    first_part, twin_near, twin_far, p, ds, scaled_q, scaled_g, factor = call(
        functools.partial(main_kernel, span, width, block_len),
        "main",
        [VMEM] * 8,
        [parts(1), parts(steps), parts(steps + 1), ((keys, rows), LOW), ((keys, rows), LOW), turned, turned, ((8, rows), F32)],
        [
            pltpu.VMEM((width + 16, keys - here), LOW),
            pltpu.VMEM((2, keys - here, pair), F32),
            pltpu.VMEM((keys // 2, width), F32),
            pltpu.VMEM((keys // 2, width), F32),
        ],
        6 * work * span,
        *(bias, qt, gt, early_vt, early_s, early_dp, early_top, late),
    )
    own_part, far_part, near_parts, far_parts = call(
        functools.partial(kept_kernel, span, width, block_len),
        "kept",
        [VMEM] * 4,
        [parts(1), parts(1), parts(steps), parts(steps)],
        [],
        work * span,
        *(p, ds, scaled_q, scaled_g),
    )

    def added(x, y):
        return (x.astype(F32) + y.astype(F32)).astype(LOW)

    from_twin_far = swapped(twin_far, 1)
    from_twin_near = swapped(twin_near, 1)
    far_back = [swapped(added(block(far_parts, i), block(from_twin_far, i)), d) for i, d in enumerate(ways)]
    near_sums = [added(block(near_parts, i), block(from_twin_near, i)) for i in range(steps)]
    far_sum = far_part.astype(F32) + block(from_twin_far, steps).astype(F32)
    for one in far_back:
        far_sum = far_sum + one.astype(F32)
    far_sum = far_sum.astype(LOW)
    near_home = [returned(first_part, 1)] + [returned(one, d) for one, d in zip(near_sums, ways)]
    far_home = moved(far_sum, -half)
    (grad_queries,) = call(
        functools.partial(query_kernel, width, block_len),
        "query",
        [pl.BlockSpec(memory_space=pl.ANY)] + [VMEM] * 4,
        [(queries.shape, LOW)],
        [],
        work * span,
        *(far_sum, ds, factor, early, late),
    )
    mine = own_part.astype(F32)
    for one in near_home + [far_home]:
        mine = mine + one.astype(F32)
    grads = mine.astype(LOW)
    return grad_queries, grads[:, :width], grads[:, width:]


def solution(mesh):
    rows = P(("outer", "inner"), None)
    body = functools.partial(shards, mesh.shape["inner"], mesh.shape["outer"])
    return jax.shard_map(
        body, mesh=mesh, in_specs=(rows, rows, rows, rows, P()), out_specs=(rows, rows, rows), check_vma=False
    )
```

```python
import functools
import math

import jax
import jax.numpy as jnp
from jax import lax
from jax.experimental import pallas as pl
from jax.experimental.pallas import tpu as pltpu
from jax.sharding import PartitionSpec as P

BLOCKED = -1e30
F32 = jnp.float32
LOW = jnp.bfloat16


def strides(span):
    return list(range(span // 2 - 2, 0, -2))


def window_ids(at, span):
    def nearest(t, u):
        return jnp.where(u < t, u, u - span)

    def same_core(t):
        others = [t ^ d for d in strides(span)]
        return [nearest(t, u) for u in others], [u - span // 2 for u in others]

    near, far = same_core(at)
    twin = at ^ 1
    twin_near, twin_far = same_core(twin)
    early = [at, at - span // 2] + near + [nearest(at, twin), twin - span // 2]
    return early, far + twin_near, twin_far


def pack_kernel(k_hbm, v_hbm, kv_ref, arrived):
    width = k_hbm.shape[1]
    copies = [
        pltpu.make_async_copy(one, kv_ref.at[:, pl.ds(i * width, width)], arrived.at[i])
        for i, one in enumerate((k_hbm, v_hbm))
    ]
    for copy in copies:
        copy.start()
    for copy in copies:
        copy.wait()


def group_passes(width, block_len, qt_ref, gt_ref, kv_ref, bias_ref, first, p_ref, dp_ref, sums_ref, top_ref, vt_ref, s_ref):
    pair = 2 * block_len
    slots = kv_ref.shape[0] // block_len
    vt_ref[:width, :] = kv_ref[:, width:].T
    vt_ref[width:, :] = jnp.ones((vt_ref.shape[0] - width, vt_ref.shape[1]), LOW)
    key_pos = lax.broadcasted_iota(jnp.int32, (block_len, pair), 0)
    row_pos = lax.broadcasted_iota(jnp.int32, (block_len, pair), 1) % block_len
    causal = key_pos <= row_pos
    scale2 = width**-0.5 * math.log2(math.e)

    def score(hp):
        lanes = slice(hp * pair, (hp + 1) * pair)
        s = jnp.dot(kv_ref[:, :width], qt_ref[:, lanes], preferred_element_type=F32)
        dp_ref[:, lanes] = jnp.dot(kv_ref[:, width:], gt_ref[:, lanes], preferred_element_type=F32)
        top = None
        for i in range(slots):
            slot = slice(i * block_len, (i + 1) * block_len)
            part = jnp.where(causal, s[slot], BLOCKED) if first + i == 0 else s[slot]
            s_ref[hp % 2, slot, :] = part
            best = jnp.max(part.reshape(-1, 8, pair), axis=0) + bias_ref[8 * (first + i) : 8 * (first + i) + 8, :]
            top = best if top is None else jnp.maximum(top, best)
        top_ref[:, lanes] = jnp.broadcast_to(jnp.max(top, axis=0, keepdims=True) * scale2, (8, pair))

    def weigh(hp):
        lanes = slice(hp * pair, (hp + 1) * pair)
        top = top_ref[0:1, lanes]
        for i in range(slots):
            slot = slice(i * block_len, (i + 1) * block_len)
            shift = bias_ref[8 * (first + i) : 8 * (first + i) + 1, :] - top
            p_ref[slot, lanes] = jnp.exp2(s_ref[hp % 2, slot, :] * scale2 + shift).astype(LOW)
        sums_ref[:, lanes] = jnp.dot(vt_ref[...], p_ref[:, lanes], preferred_element_type=F32)

    return score, weigh


def early_kernel(span, width, block_len, doc_hbm, at_ref, q_hbm, g_hbm, kv_ref, qt_ref, gt_ref, bias_ref, p_ref, dp_ref, sums_ref, top_ref, q_ref, g_ref, doc_ref, arrived, vt_ref, s_ref):
    places = enumerate(((q_hbm, q_ref), (g_hbm, g_ref), (doc_hbm, doc_ref)))
    copies = [pltpu.make_async_copy(there, here, arrived.at[i]) for i, (there, here) in places]
    for copy in copies:
        copy.start()
    pair = 2 * block_len
    score, weigh = group_passes(
        width, block_len, qt_ref, gt_ref, kv_ref, bias_ref, 0, p_ref, dp_ref, sums_ref, top_ref, vt_ref, s_ref
    )
    for copy in copies:
        copy.wait()
    at = at_ref[0]
    own_doc = doc_ref[at]
    for i, one in enumerate(sum(window_ids(at, span), [])):
        allowed = (one >= 0) & (doc_ref[jnp.maximum(one, 0)] == own_doc)
        bias_ref[8 * i : 8 * i + 8, :] = jnp.full((8, pair), jnp.where(allowed, 0.0, BLOCKED).astype(F32))
    pairs = q_ref.shape[1] // width // 2
    for hp in range(-1, pairs):
        if hp + 1 < pairs:
            for h in (2 * hp + 2, 2 * hp + 3):
                qt_ref[:, h * block_len : (h + 1) * block_len] = q_ref[:, h * width : (h + 1) * width].T
                gt_ref[:, h * block_len : (h + 1) * block_len] = g_ref[:, h * width : (h + 1) * width].T
            score(hp + 1)
        if hp >= 0:
            weigh(hp)


def middle_kernel(first, width, block_len, bias_ref, qt_ref, gt_ref, kv_ref, p_ref, dp_ref, sums_ref, top_ref, vt_ref, s_ref):
    score, weigh = group_passes(
        width, block_len, qt_ref, gt_ref, kv_ref, bias_ref, first, p_ref, dp_ref, sums_ref, top_ref, vt_ref, s_ref
    )
    pairs = qt_ref.shape[1] // block_len // 2
    for hp in range(-1, pairs):
        if hp + 1 < pairs:
            score(hp + 1)
        if hp >= 0:
            weigh(hp)


def main_kernel(span, width, block_len, *refs):
    bias_ref, qt_ref, gt_ref, kv_ref = refs[:4]
    early, middle = refs[4:8], refs[8:12]
    first_ref, twin_near_ref, twin_far_ref = refs[12:15]
    ds_refs, sq_refs, sg_refs, factor_refs = refs[15:18], refs[18:20], refs[20:22], refs[22:25]
    late, (vt_ref, s_ref, dk_ref, dv_ref) = refs[25:29], refs[29:]
    scale = width**-0.5
    pairs = qt_ref.shape[1] // block_len // 2
    pair = 2 * block_len
    steps = len(strides(span))
    groups = (early, middle, late)
    score, weigh = group_passes(
        width, block_len, qt_ref, gt_ref, kv_ref, bias_ref, span - steps, *late, vt_ref, s_ref
    )
    nt = (((1,), (1,)), ((), ()))
    twins = ((steps + 2, 2), (steps, steps), (0, steps))
    homes = [(first_ref, 0), (twin_far_ref, steps)]
    homes += [(twin_near_ref, i) for i in range(steps)] + [(twin_far_ref, i) for i in range(steps)]
    state = {}

    def rows_of(first, count):
        return slice(first * block_len, (first + count) * block_len)

    def settle(hp):
        lanes = slice(hp * pair, (hp + 1) * pair)
        tops = [top_ref[0:1, lanes] for _, _, _, top_ref in groups]
        top = functools.reduce(jnp.maximum, tops)
        shares = [jnp.exp2(one - top) for one in tops]
        sums = None
        for share, (_, _, sums_ref, _) in zip(shares, groups):
            part = sums_ref[:, lanes] * share
            sums = part if sums is None else sums + part
        inverse = 1.0 / sums[width : width + 1]
        wide_q, wide_g = qt_ref[:, lanes].astype(F32), gt_ref[:, lanes].astype(F32)
        delta = jnp.sum(sums[:width] * wide_g, axis=0, keepdims=True) * inverse
        scaled = []
        for i, share in enumerate(shares):
            factor = inverse * share
            factor_refs[i][:, lanes] = jnp.broadcast_to(factor * scale, (8, pair))
            scaled.append(((wide_q * (factor * scale)).astype(LOW), (wide_g * factor).astype(LOW)))
            if i < 2:
                sq_refs[i][:, lanes], sg_refs[i][:, lanes] = scaled[i]
        state[hp] = (delta, scaled)

    def spread(hp):
        lanes = slice(hp * pair, (hp + 1) * pair)
        delta, scaled = state[hp]
        place = 0
        for (p_ref, dp_ref, _, _), ds_ref, (sq, sg), (first, count) in zip(groups, ds_refs, scaled, twins):
            ds_ref[:, lanes] = (p_ref[:, lanes].astype(F32) * (dp_ref[:, lanes] - delta)).astype(LOW)
            rows, kept = rows_of(first, count), rows_of(place, count)
            dv = lax.dot_general(p_ref[rows, lanes], sg, nt, preferred_element_type=F32)
            dk = lax.dot_general(ds_ref[rows, lanes], sq, nt, preferred_element_type=F32)
            if hp > 0:
                dk = dk_ref[kept, :] + dk
                dv = dv_ref[kept, :] + dv
            if hp < pairs - 1:
                dk_ref[kept, :] = dk
                dv_ref[kept, :] = dv
            else:
                dk, dv = dk.astype(LOW), dv.astype(LOW)
                for i in range(count):
                    home, where = homes[place + i]
                    home[rows_of(where, 1), :width] = dk[rows_of(i, 1)]
                    home[rows_of(where, 1), width:] = dv[rows_of(i, 1)]
            place += count

    for hp in range(-2, pairs):
        if hp >= 0:
            settle(hp)
        if hp + 2 < pairs:
            score(hp + 2)
        if 0 <= hp + 1 < pairs:
            weigh(hp + 1)
        if hp >= 0:
            spread(hp)


def kept_kernel(width, *refs):
    nt = (((1,), (1,)), ((), ()))
    for p_ref, ds_ref, sq_ref, sg_ref, outs in (refs[:4] + (refs[8:11],), refs[4:8] + (refs[11:],)):
        count = sum(ref.shape[0] for ref in outs)
        dk = lax.dot_general(ds_ref[:count, :], sq_ref[...], nt, preferred_element_type=F32).astype(LOW)
        dv = lax.dot_general(p_ref[:count, :], sg_ref[...], nt, preferred_element_type=F32).astype(LOW)
        first = 0
        for ref in outs:
            ref[:, :width] = dk[first : first + ref.shape[0]]
            ref[:, width:] = dv[first : first + ref.shape[0]]
            first += ref.shape[0]


def query_kernel(width, block_len, unused_ref, *refs):
    ds_refs, factor_refs, kv_refs, dq_ref = refs[:3], refs[3:6], refs[6:9], refs[9]
    turned = [kv_ref[:, :width].T for kv_ref in kv_refs]
    pair = 2 * block_len
    for hp in range(dq_ref.shape[1] // width // 2):
        lanes = slice(hp * pair, (hp + 1) * pair)
        dq = None
        for keys, ds_ref, factor_ref in zip(turned, ds_refs, factor_refs):
            part = jnp.dot(keys, ds_ref[:, lanes], preferred_element_type=F32) * factor_ref[0:1, lanes]
            dq = part if dq is None else dq + part
        for h in range(2):
            head = slice((2 * hp + h) * width, (2 * hp + h + 1) * width)
            dq_ref[:, head] = dq[:, h * block_len : (h + 1) * block_len].T.astype(LOW)


HBM = pl.BlockSpec(memory_space=pltpu.HBM)
VMEM = pl.BlockSpec(memory_space=pltpu.VMEM)
SMEM = pl.BlockSpec(memory_space=pltpu.SMEM)


def in_hbm(x):
    return pltpu.with_memory_space_constraint(x, pltpu.HBM)


def call(body, name, ins, outs, scratch, flops, *operands):
    return pl.pallas_call(
        body,
        out_shape=tuple(jax.ShapeDtypeStruct(shape, kind) for shape, kind in outs),
        in_specs=ins,
        out_specs=(VMEM,) * len(outs),
        scratch_shapes=scratch,
        compiler_params=pltpu.CompilerParams(vmem_limit_bytes=24 * 1024 * 1024),
        cost_estimate=pl.CostEstimate(flops=flops, bytes_accessed=1 << 16, transcendentals=0),
        name=name,
    )(*operands)


def shards(inner_count, outer_count, queries, key_rows, value_rows, grad_output, doc_blocks):
    width = key_rows.shape[1]
    block_len = key_rows.shape[0]
    span = inner_count
    half = span // 2
    devices = inner_count * outer_count
    inner_at = lax.axis_index("inner")
    outer_at = lax.axis_index("outer")
    at = outer_at * inner_count + inner_at
    ways = strides(span)

    def place(t):
        return (t % inner_count) * outer_count + t // inner_count

    def moved(x, distance):
        route = [(place(t), place((t + distance) % devices)) for t in range(devices)]
        return lax.ppermute(x, ("inner", "outer"), route)

    def grouped(x, distance):
        return lax.ppermute(x, "outer", [(i, (i + distance) % outer_count) for i in range(outer_count)])

    def returned(x, d):
        route = []
        for t in range(devices):
            u = t ^ d
            route.append((place(t), place(u if u < t else (u - inner_count) % devices)))
        return lax.ppermute(x, ("inner", "outer"), route)

    def swapped(x, d):
        return lax.ppermute(x, "inner", [(i, i ^ d) for i in range(inner_count)])

    def above(d):
        return inner_at > (inner_at ^ d)

    def block(x, i):
        return x[i * block_len : (i + 1) * block_len]

    (own,) = call(
        pack_kernel,
        "pack",
        [HBM, HBM],
        [((block_len, 2 * width), LOW)],
        [pltpu.SemaphoreType.DMA((2,))],
        0,
        *(in_hbm(key_rows), in_hbm(value_rows)),
    )
    prior = grouped(own, 1)
    far = moved(own, half)
    nears = [swapped(jnp.where(above(d), prior, own), d) for d in ways]
    fars = [swapped(far, d) for d in ways[:-1]]
    nears, later_far = lax.optimization_barrier((jnp.concatenate(nears, axis=0), far))
    fars.append(swapped(later_far, ways[-1]))
    twin_first = swapped(jnp.concatenate([jnp.where(above(1), prior, own), far], axis=0), 1)
    early = jnp.concatenate([own, far, nears, twin_first], axis=0)

    steps = len(ways)
    heads = queries.shape[1] // width
    rows = heads * block_len
    pair = 2 * block_len
    work = 2 * rows * width * block_len
    turned = ((width, rows), LOW)

    def parts(n):
        return ((n * block_len, 2 * width), LOW)

    def sums_of(kv):
        keys = kv.shape[0]
        return [((keys, rows), LOW), ((keys, rows), F32), ((width + 16, rows), F32), ((8, rows), F32)]

    def scratch_of(kv):
        return [pltpu.VMEM((width + 16, kv.shape[0]), LOW), pltpu.VMEM((2, kv.shape[0], pair), F32)]

    qt, gt, bias, *early_sums = call(
        functools.partial(early_kernel, span, width, block_len),
        "early",
        [HBM, SMEM, HBM, HBM, VMEM],
        [turned, turned, ((8 * span, pair), F32)] + sums_of(early),
        [
            pltpu.VMEM(queries.shape, LOW),
            pltpu.VMEM(queries.shape, LOW),
            pltpu.SMEM(doc_blocks.shape, jnp.int32),
            pltpu.SemaphoreType.DMA((3,)),
            *scratch_of(early),
        ],
        40 * work * (steps + 4),
        *(in_hbm(doc_blocks), at.reshape(1), in_hbm(queries), in_hbm(grad_output), early),
    )
    *fars, early_sums[-1] = lax.optimization_barrier((*fars, early_sums[-1]))
    fars = jnp.concatenate(fars, axis=0)
    twin_nears, late = swapped(nears, 1), swapped(fars, 1)
    middle = jnp.concatenate([fars, twin_nears], axis=0)
    middle_sums = call(
        functools.partial(middle_kernel, steps + 4, width, block_len),
        "middle",
        [VMEM] * 4,
        sums_of(middle),
        scratch_of(middle),
        40 * work * (2 * steps),
        *(bias, qt, gt, middle),
    )
    groups = (early, middle, late)
    first_part, twin_near, twin_far, *rest = call(
        functools.partial(main_kernel, span, width, block_len),
        "main",
        [VMEM] * 12,
        [
            *(parts(1), parts(steps), parts(steps + 1)),
            *(((kv.shape[0], rows), LOW) for kv in groups),
            *([turned] * 4),
            *([((8, rows), F32)] * 3),
        ],
        [
            *(pltpu.VMEM(shape, kind) for shape, kind in sums_of(late)),
            *scratch_of(late),
            pltpu.VMEM((span // 2 * block_len, width), F32),
            pltpu.VMEM((span // 2 * block_len, width), F32),
        ],
        6 * work * span,
        *(bias, qt, gt, late, *early_sums, *middle_sums),
    )
    ds, scaled_q, scaled_g, factors = rest[:3], rest[3:5], rest[5:7], rest[7:]
    own_part, far_part, near_parts, far_parts = call(
        functools.partial(kept_kernel, width),
        "kept",
        [VMEM] * 8,
        [parts(1), parts(1), parts(steps), parts(steps)],
        [],
        work * span,
        *(early_sums[0], ds[0], scaled_q[0], scaled_g[0], middle_sums[0], ds[1], scaled_q[1], scaled_g[1]),
    )

    def added(x, y):
        return (x.astype(F32) + y.astype(F32)).astype(LOW)

    from_twin_far = swapped(twin_far, 1)
    from_twin_near = swapped(twin_near, 1)
    far_back = [swapped(added(block(far_parts, i), block(from_twin_far, i)), d) for i, d in enumerate(ways)]
    near_sums = [added(block(near_parts, i), block(from_twin_near, i)) for i in range(steps)]
    far_sum = far_part.astype(F32) + block(from_twin_far, steps).astype(F32)
    for one in far_back:
        far_sum = far_sum + one.astype(F32)
    far_sum = far_sum.astype(LOW)
    near_home = [returned(one, d) for one, d in zip(near_sums, ways)]
    far_sum, first_part = lax.optimization_barrier((far_sum, first_part))
    far_home = moved(far_sum, -half)
    first_home = returned(first_part, 1)
    (grad_queries,) = call(
        functools.partial(query_kernel, width, block_len),
        "query",
        [pl.BlockSpec(memory_space=pl.ANY)] + [VMEM] * 9,
        [(queries.shape, LOW)],
        [],
        work * span,
        *(far_sum, *ds, *factors, *groups),
    )
    mine = own_part.astype(F32)
    for one in near_home + [first_home, far_home]:
        mine = mine + one.astype(F32)
    grads = mine.astype(LOW)
    return grad_queries, grads[:, :width], grads[:, width:]


def solution(mesh):
    rows = P(("outer", "inner"), None)
    body = functools.partial(shards, mesh.shape["inner"], mesh.shape["outer"])
    return jax.shard_map(
        body, mesh=mesh, in_specs=(rows, rows, rows, rows, P()), out_specs=(rows, rows, rows), check_vma=False
    )
```

```python
import functools
import math

import jax
import jax.numpy as jnp
from jax import lax
from jax.experimental import pallas as pl
from jax.experimental.pallas import tpu as pltpu
from jax.sharding import PartitionSpec as P

BLOCKED = -1e30
F32 = jnp.float32
LOW = jnp.bfloat16


def strides(span):
    return list(range(2, span // 2, 2))


def far_strides(span):
    ways = strides(span)
    return ways[-1:] + ways[:-1]


def window_ids(at, span):
    def nearest(t, u):
        return jnp.where(u < t, u, u - span)

    def same_core(t):
        near = [nearest(t, t ^ d) for d in strides(span)]
        return near, [(t ^ d) - span // 2 for d in far_strides(span)]

    near, far = same_core(at)
    twin = at ^ 1
    twin_near, twin_far = same_core(twin)
    return [at, at - span // 2] + near, far + [nearest(at, twin), twin - span // 2] + twin_near, twin_far


def pack_kernel(k_hbm, v_hbm, kv_ref, arrived):
    width = k_hbm.shape[1]
    copies = [
        pltpu.make_async_copy(one, kv_ref.at[:, pl.ds(i * width, width)], arrived.at[i])
        for i, one in enumerate((k_hbm, v_hbm))
    ]
    for copy in copies:
        copy.start()
    for copy in copies:
        copy.wait()


def group_passes(width, block_len, qt_ref, gt_ref, kv_ref, bias_ref, first, p_ref, dp_ref, sums_ref, top_ref, vt_ref, s_ref):
    pair = 2 * block_len
    slots = kv_ref.shape[0] // block_len
    vt_ref[:width, :] = kv_ref[:, width:].T
    vt_ref[width:, :] = jnp.ones((vt_ref.shape[0] - width, vt_ref.shape[1]), LOW)
    key_pos = lax.broadcasted_iota(jnp.int32, (block_len, pair), 0)
    row_pos = lax.broadcasted_iota(jnp.int32, (block_len, pair), 1) % block_len
    causal = key_pos <= row_pos
    scale2 = width**-0.5 * math.log2(math.e)

    def score(hp):
        lanes = slice(hp * pair, (hp + 1) * pair)
        s = jnp.dot(kv_ref[:, :width], qt_ref[:, lanes], preferred_element_type=F32)
        dp_ref[:, lanes] = jnp.dot(kv_ref[:, width:], gt_ref[:, lanes], preferred_element_type=F32)
        top = None
        for i in range(slots):
            slot = slice(i * block_len, (i + 1) * block_len)
            part = jnp.where(causal, s[slot], BLOCKED) if first + i == 0 else s[slot]
            s_ref[hp % 2, slot, :] = part
            best = jnp.max(part.reshape(-1, 8, pair), axis=0) + bias_ref[8 * (first + i) : 8 * (first + i) + 8, :]
            top = best if top is None else jnp.maximum(top, best)
        top_ref[:, lanes] = jnp.broadcast_to(jnp.max(top, axis=0, keepdims=True) * scale2, (8, pair))

    def weigh(hp):
        lanes = slice(hp * pair, (hp + 1) * pair)
        top = top_ref[0:1, lanes]
        for i in range(slots):
            slot = slice(i * block_len, (i + 1) * block_len)
            shift = bias_ref[8 * (first + i) : 8 * (first + i) + 1, :] - top
            p_ref[slot, lanes] = jnp.exp2(s_ref[hp % 2, slot, :] * scale2 + shift).astype(LOW)
        sums_ref[:, lanes] = jnp.dot(vt_ref[...], p_ref[:, lanes], preferred_element_type=F32)

    return score, weigh


def early_kernel(span, width, block_len, doc_hbm, at_ref, q_hbm, g_hbm, kv_ref, qt_ref, gt_ref, bias_ref, p_ref, dp_ref, sums_ref, top_ref, q_ref, g_ref, doc_ref, arrived, vt_ref, s_ref):
    places = enumerate(((q_hbm, q_ref), (g_hbm, g_ref), (doc_hbm, doc_ref)))
    copies = [pltpu.make_async_copy(there, here, arrived.at[i]) for i, (there, here) in places]
    for copy in copies:
        copy.start()
    pair = 2 * block_len
    score, weigh = group_passes(
        width, block_len, qt_ref, gt_ref, kv_ref, bias_ref, 0, p_ref, dp_ref, sums_ref, top_ref, vt_ref, s_ref
    )
    for copy in copies:
        copy.wait()
    at = at_ref[0]
    own_doc = doc_ref[at]
    for i, one in enumerate(sum(window_ids(at, span), [])):
        allowed = (one >= 0) & (doc_ref[jnp.maximum(one, 0)] == own_doc)
        bias_ref[8 * i : 8 * i + 8, :] = jnp.full((8, pair), jnp.where(allowed, 0.0, BLOCKED).astype(F32))
    pairs = q_ref.shape[1] // width // 2
    for hp in range(-1, pairs):
        if hp + 1 < pairs:
            for h in (2 * hp + 2, 2 * hp + 3):
                qt_ref[:, h * block_len : (h + 1) * block_len] = q_ref[:, h * width : (h + 1) * width].T
                gt_ref[:, h * block_len : (h + 1) * block_len] = g_ref[:, h * width : (h + 1) * width].T
            score(hp + 1)
        if hp >= 0:
            weigh(hp)


def middle_kernel(first, width, block_len, bias_ref, qt_ref, gt_ref, kv_ref, p_ref, dp_ref, sums_ref, top_ref, vt_ref, s_ref):
    score, weigh = group_passes(
        width, block_len, qt_ref, gt_ref, kv_ref, bias_ref, first, p_ref, dp_ref, sums_ref, top_ref, vt_ref, s_ref
    )
    pairs = qt_ref.shape[1] // block_len // 2
    for hp in range(-1, pairs):
        if hp + 1 < pairs:
            score(hp + 1)
        if hp >= 0:
            weigh(hp)


def main_kernel(span, width, block_len, *refs):
    bias_ref, qt_ref, gt_ref, kv_ref = refs[:4]
    early, middle = refs[4:8], refs[8:12]
    first_ref, twin_near_ref, twin_far_ref = refs[12:15]
    ds_refs, sq_refs, sg_refs, factor_refs = refs[15:18], refs[18:20], refs[20:22], refs[22:25]
    late, (vt_ref, s_ref, dk_ref, dv_ref) = refs[25:29], refs[29:]
    scale = width**-0.5
    pairs = qt_ref.shape[1] // block_len // 2
    pair = 2 * block_len
    steps = len(strides(span))
    groups = (early, middle, late)
    score, weigh = group_passes(
        width, block_len, qt_ref, gt_ref, kv_ref, bias_ref, span - steps, *late, vt_ref, s_ref
    )
    nt = (((1,), (1,)), ((), ()))
    twins = ((0, 0), (steps, steps + 2), (0, steps))
    homes = [(first_ref, 0), (twin_far_ref, steps)]
    homes += [(twin_near_ref, i) for i in range(steps)] + [(twin_far_ref, i) for i in range(steps)]
    state = {}

    def rows_of(first, count):
        return slice(first * block_len, (first + count) * block_len)

    def settle(hp):
        lanes = slice(hp * pair, (hp + 1) * pair)
        tops = [top_ref[0:1, lanes] for _, _, _, top_ref in groups]
        top = functools.reduce(jnp.maximum, tops)
        shares = [jnp.exp2(one - top) for one in tops]
        sums = None
        for share, (_, _, sums_ref, _) in zip(shares, groups):
            part = sums_ref[:, lanes] * share
            sums = part if sums is None else sums + part
        inverse = 1.0 / sums[width : width + 1]
        wide_q, wide_g = qt_ref[:, lanes].astype(F32), gt_ref[:, lanes].astype(F32)
        delta = jnp.sum(sums[:width] * wide_g, axis=0, keepdims=True) * inverse
        scaled = []
        for i, share in enumerate(shares):
            factor = inverse * share
            factor_refs[i][:, lanes] = jnp.broadcast_to(factor * scale, (8, pair))
            scaled.append(((wide_q * (factor * scale)).astype(LOW), (wide_g * factor).astype(LOW)))
            if i < 2:
                sq_refs[i][:, lanes], sg_refs[i][:, lanes] = scaled[i]
        state[hp] = (delta, scaled)

    def spread(hp):
        lanes = slice(hp * pair, (hp + 1) * pair)
        delta, scaled = state[hp]
        place = 0
        for (p_ref, dp_ref, _, _), ds_ref, (sq, sg), (first, count) in zip(groups, ds_refs, scaled, twins):
            ds_ref[:, lanes] = (p_ref[:, lanes].astype(F32) * (dp_ref[:, lanes] - delta)).astype(LOW)
            if not count:
                continue
            rows, kept = rows_of(first, count), rows_of(place, count)
            dv = lax.dot_general(p_ref[rows, lanes], sg, nt, preferred_element_type=F32)
            dk = lax.dot_general(ds_ref[rows, lanes], sq, nt, preferred_element_type=F32)
            if hp > 0:
                dk = dk_ref[kept, :] + dk
                dv = dv_ref[kept, :] + dv
            if hp < pairs - 1:
                dk_ref[kept, :] = dk
                dv_ref[kept, :] = dv
            else:
                dk, dv = dk.astype(LOW), dv.astype(LOW)
                for i in range(count):
                    home, where = homes[place + i]
                    home[rows_of(where, 1), :width] = dk[rows_of(i, 1)]
                    home[rows_of(where, 1), width:] = dv[rows_of(i, 1)]
            place += count

    for hp in range(-2, pairs):
        if hp >= 0:
            settle(hp)
        if hp + 2 < pairs:
            score(hp + 2)
        if 0 <= hp + 1 < pairs:
            weigh(hp + 1)
        if hp >= 0:
            spread(hp)


def kept_kernel(width, *refs):
    nt = (((1,), (1,)), ((), ()))
    for p_ref, ds_ref, sq_ref, sg_ref, outs in (refs[:4] + (refs[8:11],), refs[4:8] + (refs[11:],)):
        count = sum(ref.shape[0] for ref in outs)
        dk = lax.dot_general(ds_ref[:count, :], sq_ref[...], nt, preferred_element_type=F32).astype(LOW)
        dv = lax.dot_general(p_ref[:count, :], sg_ref[...], nt, preferred_element_type=F32).astype(LOW)
        first = 0
        for ref in outs:
            ref[:, :width] = dk[first : first + ref.shape[0]]
            ref[:, width:] = dv[first : first + ref.shape[0]]
            first += ref.shape[0]


def query_kernel(width, block_len, unused_ref, *refs):
    ds_refs, factor_refs, kv_refs, dq_ref = refs[:3], refs[3:6], refs[6:9], refs[9]
    turned = [kv_ref[:, :width].T for kv_ref in kv_refs]
    pair = 2 * block_len
    for hp in range(dq_ref.shape[1] // width // 2):
        lanes = slice(hp * pair, (hp + 1) * pair)
        dq = None
        for keys, ds_ref, factor_ref in zip(turned, ds_refs, factor_refs):
            part = jnp.dot(keys, ds_ref[:, lanes], preferred_element_type=F32) * factor_ref[0:1, lanes]
            dq = part if dq is None else dq + part
        for h in range(2):
            head = slice((2 * hp + h) * width, (2 * hp + h + 1) * width)
            dq_ref[:, head] = dq[:, h * block_len : (h + 1) * block_len].T.astype(LOW)


HBM = pl.BlockSpec(memory_space=pltpu.HBM)
VMEM = pl.BlockSpec(memory_space=pltpu.VMEM)
SMEM = pl.BlockSpec(memory_space=pltpu.SMEM)


def in_hbm(x):
    return pltpu.with_memory_space_constraint(x, pltpu.HBM)


def call(body, name, ins, outs, scratch, flops, *operands):
    return pl.pallas_call(
        body,
        out_shape=tuple(jax.ShapeDtypeStruct(shape, kind) for shape, kind in outs),
        in_specs=ins,
        out_specs=(VMEM,) * len(outs),
        scratch_shapes=scratch,
        compiler_params=pltpu.CompilerParams(vmem_limit_bytes=24 * 1024 * 1024),
        cost_estimate=pl.CostEstimate(flops=flops, bytes_accessed=1 << 16, transcendentals=0),
        name=name,
    )(*operands)


def shards(inner_count, outer_count, queries, key_rows, value_rows, grad_output, doc_blocks):
    width = key_rows.shape[1]
    block_len = key_rows.shape[0]
    span = inner_count
    half = span // 2
    devices = inner_count * outer_count
    inner_at = lax.axis_index("inner")
    outer_at = lax.axis_index("outer")
    at = outer_at * inner_count + inner_at
    ways, far_ways = strides(span), far_strides(span)

    def place(t):
        return (t % inner_count) * outer_count + t // inner_count

    def moved(x, distance):
        route = [(place(t), place((t + distance) % devices)) for t in range(devices)]
        return lax.ppermute(x, ("inner", "outer"), route)

    def grouped(x, distance):
        return lax.ppermute(x, "outer", [(i, (i + distance) % outer_count) for i in range(outer_count)])

    def returned(x, d):
        route = []
        for t in range(devices):
            u = t ^ d
            route.append((place(t), place(u if u < t else (u - inner_count) % devices)))
        return lax.ppermute(x, ("inner", "outer"), route)

    def swapped(x, d):
        return lax.ppermute(x, "inner", [(i, i ^ d) for i in range(inner_count)])

    def above(d):
        return inner_at > (inner_at ^ d)

    def block(x, i):
        return x[i * block_len : (i + 1) * block_len]

    (own,) = call(
        pack_kernel,
        "pack",
        [HBM, HBM],
        [((block_len, 2 * width), LOW)],
        [pltpu.SemaphoreType.DMA((2,))],
        0,
        *(in_hbm(key_rows), in_hbm(value_rows)),
    )
    prior = grouped(own, 1)
    far = moved(own, half)
    nears = [swapped(jnp.where(above(d), prior, own), d) for d in ways]
    fars = [swapped(far, d) for d in far_ways[:-1]]
    nears[1], later_far = lax.optimization_barrier((nears[1], far))
    nears = jnp.concatenate(nears, axis=0)
    fars.append(swapped(later_far, far_ways[-1]))
    early = jnp.concatenate([own, far, nears], axis=0)
    for_twin = jnp.concatenate([jnp.where(above(1), prior, own), far, nears], axis=0)

    steps = len(ways)
    heads = queries.shape[1] // width
    rows = heads * block_len
    pair = 2 * block_len
    work = 2 * rows * width * block_len
    turned = ((width, rows), LOW)

    def parts(n):
        return ((n * block_len, 2 * width), LOW)

    def sums_of(kv):
        keys = kv.shape[0]
        return [((keys, rows), LOW), ((keys, rows), F32), ((width + 16, rows), F32), ((8, rows), F32)]

    def scratch_of(kv):
        return [pltpu.VMEM((width + 16, kv.shape[0]), LOW), pltpu.VMEM((2, kv.shape[0], pair), F32)]

    qt, gt, bias, *early_sums = call(
        functools.partial(early_kernel, span, width, block_len),
        "early",
        [HBM, SMEM, HBM, HBM, VMEM],
        [turned, turned, ((8 * span, pair), F32)] + sums_of(early),
        [
            pltpu.VMEM(queries.shape, LOW),
            pltpu.VMEM(queries.shape, LOW),
            pltpu.SMEM(doc_blocks.shape, jnp.int32),
            pltpu.SemaphoreType.DMA((3,)),
            *scratch_of(early),
        ],
        40 * work * (steps + 2),
        *(in_hbm(doc_blocks), at.reshape(1), in_hbm(queries), in_hbm(grad_output), early),
    )
    *fars, early_sums[-1] = lax.optimization_barrier((*fars, early_sums[-1]))
    fars = jnp.concatenate(fars, axis=0)
    from_twin, late = swapped(for_twin, 1), swapped(fars, 1)
    middle = jnp.concatenate([fars, from_twin], axis=0)
    middle_sums = call(
        functools.partial(middle_kernel, steps + 2, width, block_len),
        "middle",
        [VMEM] * 4,
        sums_of(middle),
        scratch_of(middle),
        40 * work * (2 * steps + 2),
        *(bias, qt, gt, middle),
    )
    groups = (early, middle, late)
    first_part, twin_near, twin_far, *rest = call(
        functools.partial(main_kernel, span, width, block_len),
        "main",
        [VMEM] * 12,
        [
            *(parts(1), parts(steps), parts(steps + 1)),
            *(((kv.shape[0], rows), LOW) for kv in groups),
            *([turned] * 4),
            *([((8, rows), F32)] * 3),
        ],
        [
            *(pltpu.VMEM(shape, kind) for shape, kind in sums_of(late)),
            *scratch_of(late),
            pltpu.VMEM((span // 2 * block_len, width), F32),
            pltpu.VMEM((span // 2 * block_len, width), F32),
        ],
        6 * work * span,
        *(bias, qt, gt, late, *early_sums, *middle_sums),
    )
    ds, scaled_q, scaled_g, factors = rest[:3], rest[3:5], rest[5:7], rest[7:]
    own_part, far_part, near_parts, far_parts = call(
        functools.partial(kept_kernel, width),
        "kept",
        [VMEM] * 8,
        [parts(1), parts(1), parts(steps), parts(steps)],
        [],
        work * span,
        *(early_sums[0], ds[0], scaled_q[0], scaled_g[0], middle_sums[0], ds[1], scaled_q[1], scaled_g[1]),
    )

    def added(x, y):
        return (x.astype(F32) + y.astype(F32)).astype(LOW)

    from_twin_far = swapped(twin_far, 1)
    from_twin_near = swapped(twin_near, 1)
    far_sums = [added(block(far_parts, i), block(from_twin_far, i)) for i in range(steps)]
    far_back = [swapped(far_sums[far_ways.index(d)], d) for d in reversed(ways)]
    near_sums = [added(block(near_parts, i), block(from_twin_near, i)) for i in range(steps)]
    far_sum = far_part.astype(F32) + block(from_twin_far, steps).astype(F32)
    for one in far_back:
        far_sum = far_sum + one.astype(F32)
    far_sum = far_sum.astype(LOW)
    near_home = [returned(near_sums[ways.index(d)], d) for d in reversed(ways)]
    far_sum, first_part = lax.optimization_barrier((far_sum, first_part))
    far_home = moved(far_sum, -half)
    first_home = returned(first_part, 1)
    (grad_queries,) = call(
        functools.partial(query_kernel, width, block_len),
        "query",
        [pl.BlockSpec(memory_space=pl.ANY)] + [VMEM] * 9,
        [(queries.shape, LOW)],
        [],
        work * span,
        *(far_sum, *ds, *factors, *groups),
    )
    mine = own_part.astype(F32)
    for one in near_home + [first_home, far_home]:
        mine = mine + one.astype(F32)
    grads = mine.astype(LOW)
    return grad_queries, grads[:, :width], grads[:, width:]


def solution(mesh):
    rows = P(("outer", "inner"), None)
    body = functools.partial(shards, mesh.shape["inner"], mesh.shape["outer"])
    return jax.shard_map(
        body, mesh=mesh, in_specs=(rows, rows, rows, rows, P()), out_specs=(rows, rows, rows), check_vma=False
    )
```

```python
import functools
import math

import jax
import jax.numpy as jnp
from jax import lax
from jax.experimental import pallas as pl
from jax.experimental.pallas import tpu as pltpu
from jax.sharding import PartitionSpec as P

BLOCKED = -1e30
F32 = jnp.float32
LOW = jnp.bfloat16


def strides(span):
    return list(range(2, span // 2, 2))


def far_strides(span):
    ways = strides(span)
    return ways[-1:] + ways[:-1]


def window_ids(at, span):
    def nearest(t, u):
        return jnp.where(u < t, u, u - span)

    def same_core(t):
        near = [nearest(t, t ^ d) for d in strides(span)]
        return near, [(t ^ d) - span // 2 for d in far_strides(span)]

    near, far = same_core(at)
    twin = at ^ 1
    twin_near, twin_far = same_core(twin)
    return [at, at - span // 2] + near, far + [nearest(at, twin), twin - span // 2] + twin_near, twin_far


def pack_kernel(k_hbm, v_hbm, kv_ref, arrived):
    width = k_hbm.shape[1]
    copies = [
        pltpu.make_async_copy(one, kv_ref.at[:, pl.ds(i * width, width)], arrived.at[i])
        for i, one in enumerate((k_hbm, v_hbm))
    ]
    for copy in copies:
        copy.start()
    for copy in copies:
        copy.wait()


def group_passes(width, block_len, qt_ref, gt_ref, kv_ref, bias_ref, first, p_ref, dp_ref, sums_ref, top_ref, vt_ref, s_ref):
    pair = 2 * block_len
    slots = kv_ref.shape[0] // block_len
    vt_ref[:width, :] = kv_ref[:, width:].T
    vt_ref[width:, :] = jnp.ones((vt_ref.shape[0] - width, vt_ref.shape[1]), LOW)
    key_pos = lax.broadcasted_iota(jnp.int32, (block_len, pair), 0)
    row_pos = lax.broadcasted_iota(jnp.int32, (block_len, pair), 1) % block_len
    causal = key_pos <= row_pos
    scale2 = width**-0.5 * math.log2(math.e)

    def score(hp):
        lanes = slice(hp * pair, (hp + 1) * pair)
        s = jnp.dot(kv_ref[:, :width], qt_ref[:, lanes], preferred_element_type=F32)
        dp_ref[:, lanes] = jnp.dot(kv_ref[:, width:], gt_ref[:, lanes], preferred_element_type=F32)
        top = None
        for i in range(slots):
            slot = slice(i * block_len, (i + 1) * block_len)
            part = jnp.where(causal, s[slot], BLOCKED) if first + i == 0 else s[slot]
            s_ref[hp % 2, slot, :] = part
            best = jnp.max(part.reshape(-1, 8, pair), axis=0) + bias_ref[8 * (first + i) : 8 * (first + i) + 8, :]
            top = best if top is None else jnp.maximum(top, best)
        top_ref[:, lanes] = jnp.broadcast_to(jnp.max(top, axis=0, keepdims=True) * scale2, (8, pair))

    def weigh(hp):
        lanes = slice(hp * pair, (hp + 1) * pair)
        top = top_ref[0:1, lanes]
        for i in range(slots):
            slot = slice(i * block_len, (i + 1) * block_len)
            shift = bias_ref[8 * (first + i) : 8 * (first + i) + 1, :] - top
            p_ref[slot, lanes] = jnp.exp2(s_ref[hp % 2, slot, :] * scale2 + shift).astype(LOW)
        sums_ref[:, lanes] = jnp.dot(vt_ref[...], p_ref[:, lanes], preferred_element_type=F32)

    return score, weigh


def early_kernel(span, width, block_len, doc_hbm, at_ref, q_hbm, g_hbm, kv_ref, qt_ref, gt_ref, bias_ref, p_ref, dp_ref, sums_ref, top_ref, q_ref, g_ref, doc_ref, arrived, vt_ref, s_ref):
    places = enumerate(((q_hbm, q_ref), (g_hbm, g_ref), (doc_hbm, doc_ref)))
    copies = [pltpu.make_async_copy(there, here, arrived.at[i]) for i, (there, here) in places]
    for copy in copies:
        copy.start()
    pair = 2 * block_len
    score, weigh = group_passes(
        width, block_len, qt_ref, gt_ref, kv_ref, bias_ref, 0, p_ref, dp_ref, sums_ref, top_ref, vt_ref, s_ref
    )
    for copy in copies:
        copy.wait()
    at = at_ref[0]
    own_doc = doc_ref[at]
    for i, one in enumerate(sum(window_ids(at, span), [])):
        allowed = (one >= 0) & (doc_ref[jnp.maximum(one, 0)] == own_doc)
        bias_ref[8 * i : 8 * i + 8, :] = jnp.full((8, pair), jnp.where(allowed, 0.0, BLOCKED).astype(F32))
    pairs = q_ref.shape[1] // width // 2
    for hp in range(-1, pairs):
        if hp + 1 < pairs:
            for h in (2 * hp + 2, 2 * hp + 3):
                qt_ref[:, h * block_len : (h + 1) * block_len] = q_ref[:, h * width : (h + 1) * width].T
                gt_ref[:, h * block_len : (h + 1) * block_len] = g_ref[:, h * width : (h + 1) * width].T
            score(hp + 1)
        if hp >= 0:
            weigh(hp)


def middle_kernel(first, width, block_len, bias_ref, qt_ref, gt_ref, kv_ref, p_ref, dp_ref, sums_ref, top_ref, vt_ref, s_ref):
    score, weigh = group_passes(
        width, block_len, qt_ref, gt_ref, kv_ref, bias_ref, first, p_ref, dp_ref, sums_ref, top_ref, vt_ref, s_ref
    )
    pairs = qt_ref.shape[1] // block_len // 2
    for hp in range(-1, pairs):
        if hp + 1 < pairs:
            score(hp + 1)
        if hp >= 0:
            weigh(hp)


def main_kernel(span, width, block_len, *refs):
    bias_ref, qt_ref, gt_ref, kv_ref = refs[:4]
    early, middle = refs[4:8], refs[8:12]
    first_ref, twin_near_ref, twin_far_ref = refs[12:15]
    ds_refs, sq_refs, sg_refs, factor_refs = refs[15:18], refs[18:20], refs[20:22], refs[22:25]
    late, (vt_ref, s_ref, dk_ref, dv_ref) = refs[25:29], refs[29:]
    scale = width**-0.5
    pairs = qt_ref.shape[1] // block_len // 2
    pair = 2 * block_len
    steps = len(strides(span))
    groups = (early, middle, late)
    score, weigh = group_passes(
        width, block_len, qt_ref, gt_ref, kv_ref, bias_ref, span - steps, *late, vt_ref, s_ref
    )
    nt = (((1,), (1,)), ((), ()))
    twins = ((0, 0), (steps, steps + 2), (0, steps))
    homes = [(first_ref, 0), (twin_far_ref, steps)]
    homes += [(twin_near_ref, i) for i in range(steps)] + [(twin_far_ref, i) for i in range(steps)]
    state = {}

    def rows_of(first, count):
        return slice(first * block_len, (first + count) * block_len)

    def settle(hp):
        lanes = slice(hp * pair, (hp + 1) * pair)
        tops = [top_ref[0:1, lanes] for _, _, _, top_ref in groups]
        top = functools.reduce(jnp.maximum, tops)
        shares = [jnp.exp2(one - top) for one in tops]
        sums = None
        for share, (_, _, sums_ref, _) in zip(shares, groups):
            part = sums_ref[:, lanes] * share
            sums = part if sums is None else sums + part
        inverse = 1.0 / sums[width : width + 1]
        wide_q, wide_g = qt_ref[:, lanes].astype(F32), gt_ref[:, lanes].astype(F32)
        delta = jnp.sum(sums[:width] * wide_g, axis=0, keepdims=True) * inverse
        scaled = []
        for i, share in enumerate(shares):
            factor = inverse * share
            factor_refs[i][:, lanes] = jnp.broadcast_to(factor * scale, (8, pair))
            scaled.append(((wide_q * (factor * scale)).astype(LOW), (wide_g * factor).astype(LOW)))
            if i < 2:
                sq_refs[i][:, lanes], sg_refs[i][:, lanes] = scaled[i]
        state[hp] = (delta, scaled)

    def spread(hp):
        lanes = slice(hp * pair, (hp + 1) * pair)
        delta, scaled = state[hp]
        place = 0
        for (p_ref, dp_ref, _, _), ds_ref, (sq, sg), (first, count) in zip(groups, ds_refs, scaled, twins):
            ds_ref[:, lanes] = (p_ref[:, lanes].astype(F32) * (dp_ref[:, lanes] - delta)).astype(LOW)
            if not count:
                continue
            rows, kept = rows_of(first, count), rows_of(place, count)
            dv = lax.dot_general(p_ref[rows, lanes], sg, nt, preferred_element_type=F32)
            dk = lax.dot_general(ds_ref[rows, lanes], sq, nt, preferred_element_type=F32)
            if hp > 0:
                dk = dk_ref[kept, :] + dk
                dv = dv_ref[kept, :] + dv
            if hp < pairs - 1:
                dk_ref[kept, :] = dk
                dv_ref[kept, :] = dv
            else:
                dk, dv = dk.astype(LOW), dv.astype(LOW)
                for i in range(count):
                    home, where = homes[place + i]
                    home[rows_of(where, 1), :width] = dk[rows_of(i, 1)]
                    home[rows_of(where, 1), width:] = dv[rows_of(i, 1)]
            place += count

    for hp in range(-2, pairs):
        if hp >= 0:
            settle(hp)
        if hp + 2 < pairs:
            score(hp + 2)
        if 0 <= hp + 1 < pairs:
            weigh(hp + 1)
        if hp >= 0:
            spread(hp)


def kept_kernel(width, *refs):
    nt = (((1,), (1,)), ((), ()))
    for p_ref, ds_ref, sq_ref, sg_ref, outs in (refs[:4] + (refs[8:11],), refs[4:8] + (refs[11:],)):
        count = sum(ref.shape[0] for ref in outs)
        dk = lax.dot_general(ds_ref[:count, :], sq_ref[...], nt, preferred_element_type=F32).astype(LOW)
        dv = lax.dot_general(p_ref[:count, :], sg_ref[...], nt, preferred_element_type=F32).astype(LOW)
        first = 0
        for ref in outs:
            ref[:, :width] = dk[first : first + ref.shape[0]]
            ref[:, width:] = dv[first : first + ref.shape[0]]
            first += ref.shape[0]


def query_kernel(width, block_len, unused_ref, *refs):
    ds_refs, factor_refs, kv_refs, dq_ref = refs[:3], refs[3:6], refs[6:9], refs[9]
    turned = [kv_ref[:, :width].T for kv_ref in kv_refs]
    pair = 2 * block_len
    for hp in range(dq_ref.shape[1] // width // 2):
        lanes = slice(hp * pair, (hp + 1) * pair)
        dq = None
        for keys, ds_ref, factor_ref in zip(turned, ds_refs, factor_refs):
            part = jnp.dot(keys, ds_ref[:, lanes], preferred_element_type=F32) * factor_ref[0:1, lanes]
            dq = part if dq is None else dq + part
        for h in range(2):
            head = slice((2 * hp + h) * width, (2 * hp + h + 1) * width)
            dq_ref[:, head] = dq[:, h * block_len : (h + 1) * block_len].T.astype(LOW)


HBM = pl.BlockSpec(memory_space=pltpu.HBM)
VMEM = pl.BlockSpec(memory_space=pltpu.VMEM)
SMEM = pl.BlockSpec(memory_space=pltpu.SMEM)


def in_hbm(x):
    return pltpu.with_memory_space_constraint(x, pltpu.HBM)


def call(body, name, ins, outs, scratch, flops, *operands):
    return pl.pallas_call(
        body,
        out_shape=tuple(jax.ShapeDtypeStruct(shape, kind) for shape, kind in outs),
        in_specs=ins,
        out_specs=(VMEM,) * len(outs),
        scratch_shapes=scratch,
        compiler_params=pltpu.CompilerParams(vmem_limit_bytes=24 * 1024 * 1024),
        cost_estimate=pl.CostEstimate(flops=flops, bytes_accessed=1 << 16, transcendentals=0),
        name=name,
    )(*operands)


def shards(inner_count, outer_count, queries, key_rows, value_rows, grad_output, doc_blocks):
    width = key_rows.shape[1]
    block_len = key_rows.shape[0]
    span = inner_count
    half = span // 2
    devices = inner_count * outer_count
    inner_at = lax.axis_index("inner")
    outer_at = lax.axis_index("outer")
    at = outer_at * inner_count + inner_at
    ways, far_ways = strides(span), far_strides(span)

    def place(t):
        return (t % inner_count) * outer_count + t // inner_count

    def moved(x, distance):
        route = [(place(t), place((t + distance) % devices)) for t in range(devices)]
        return lax.ppermute(x, ("inner", "outer"), route)

    def grouped(x, distance):
        return lax.ppermute(x, "outer", [(i, (i + distance) % outer_count) for i in range(outer_count)])

    def returned(x, d):
        route = []
        for t in range(devices):
            u = t ^ d
            route.append((place(t), place(u if u < t else (u - inner_count) % devices)))
        return lax.ppermute(x, ("inner", "outer"), route)

    def swapped(x, d):
        return lax.ppermute(x, "inner", [(i, i ^ d) for i in range(inner_count)])

    def above(d):
        return inner_at > (inner_at ^ d)

    def block(x, i):
        return x[i * block_len : (i + 1) * block_len]

    (own,) = call(
        pack_kernel,
        "pack",
        [HBM, HBM],
        [((block_len, 2 * width), LOW)],
        [pltpu.SemaphoreType.DMA((2,))],
        0,
        *(in_hbm(key_rows), in_hbm(value_rows)),
    )
    prior = grouped(own, 1)
    far = moved(own, half)
    nears = [swapped(jnp.where(above(d), prior, own), d) for d in ways]
    fars = [swapped(far, d) for d in far_ways[:-1]]
    nears[1], later_far = lax.optimization_barrier((nears[1], far))
    nears = jnp.concatenate(nears, axis=0)
    fars.append(swapped(later_far, far_ways[-1]))
    early = jnp.concatenate([own, far, nears], axis=0)
    for_twin = jnp.concatenate([jnp.where(above(1), prior, own), far, nears], axis=0)

    steps = len(ways)
    heads = queries.shape[1] // width
    rows = heads * block_len
    pair = 2 * block_len
    work = 2 * rows * width * block_len
    turned = ((width, rows), LOW)

    def parts(n):
        return ((n * block_len, 2 * width), LOW)

    def sums_of(kv):
        keys = kv.shape[0]
        return [((keys, rows), LOW), ((keys, rows), F32), ((width + 16, rows), F32), ((8, rows), F32)]

    def scratch_of(kv):
        return [pltpu.VMEM((width + 16, kv.shape[0]), LOW), pltpu.VMEM((2, kv.shape[0], pair), F32)]

    qt, gt, bias, *early_sums = call(
        functools.partial(early_kernel, span, width, block_len),
        "early",
        [HBM, SMEM, HBM, HBM, VMEM],
        [turned, turned, ((8 * span, pair), F32)] + sums_of(early),
        [
            pltpu.VMEM(queries.shape, LOW),
            pltpu.VMEM(queries.shape, LOW),
            pltpu.SMEM(doc_blocks.shape, jnp.int32),
            pltpu.SemaphoreType.DMA((3,)),
            *scratch_of(early),
        ],
        40 * work * (steps + 2),
        *(in_hbm(doc_blocks), at.reshape(1), in_hbm(queries), in_hbm(grad_output), early),
    )
    *fars, early_sums[-1] = lax.optimization_barrier((*fars, early_sums[-1]))
    fars = jnp.concatenate(fars, axis=0)
    from_twin, late = swapped(for_twin, 1), swapped(fars, 1)
    middle = jnp.concatenate([fars, from_twin], axis=0)
    middle_sums = call(
        functools.partial(middle_kernel, steps + 2, width, block_len),
        "middle",
        [VMEM] * 4,
        sums_of(middle),
        scratch_of(middle),
        40 * work * (2 * steps + 2),
        *(bias, qt, gt, middle),
    )
    groups = (early, middle, late)
    first_part, twin_near, twin_far, *rest = call(
        functools.partial(main_kernel, span, width, block_len),
        "main",
        [VMEM] * 12,
        [
            *(parts(1), parts(steps), parts(steps + 1)),
            *(((kv.shape[0], rows), LOW) for kv in groups),
            *([turned] * 4),
            *([((8, rows), F32)] * 3),
        ],
        [
            *(pltpu.VMEM(shape, kind) for shape, kind in sums_of(late)),
            *scratch_of(late),
            pltpu.VMEM((span // 2 * block_len, width), F32),
            pltpu.VMEM((span // 2 * block_len, width), F32),
        ],
        6 * work * span,
        *(bias, qt, gt, late, *early_sums, *middle_sums),
    )
    ds, scaled_q, scaled_g, factors = rest[:3], rest[3:5], rest[5:7], rest[7:]
    own_part, far_part, near_parts, far_parts = call(
        functools.partial(kept_kernel, width),
        "kept",
        [VMEM] * 8,
        [parts(1), parts(1), parts(steps), parts(steps)],
        [],
        work * span,
        *(early_sums[0], ds[0], scaled_q[0], scaled_g[0], middle_sums[0], ds[1], scaled_q[1], scaled_g[1]),
    )

    def added(x, y):
        return (x.astype(F32) + y.astype(F32)).astype(LOW)

    from_twin_far = swapped(twin_far, 1)
    from_twin_near = swapped(twin_near, 1)
    far_sums = [added(block(far_parts, i), block(from_twin_far, i)) for i in range(steps)]
    far_back = [swapped(far_sums[far_ways.index(d)], d) for d in reversed(ways)]
    near_sums = [added(block(near_parts, i), block(from_twin_near, i)) for i in range(steps)]
    far_sum = far_part.astype(F32) + block(from_twin_far, steps).astype(F32)
    for one in far_back:
        far_sum = far_sum + one.astype(F32)
    far_sum = far_sum.astype(LOW)
    near_home = [returned(near_sums[ways.index(d)], d) for d in reversed(ways)]
    far_sum, first_part = lax.optimization_barrier((far_sum, first_part))
    far_home = moved(far_sum, -half)
    first_home = returned(first_part, 1)
    (grad_queries,) = call(
        functools.partial(query_kernel, width, block_len),
        "query",
        [pl.BlockSpec(memory_space=pl.ANY)] + [VMEM] * 9,
        [(queries.shape, LOW)],
        [],
        work * span,
        *(first_part, *ds, *factors, *groups),
    )
    mine = own_part.astype(F32)
    for one in near_home + [first_home, far_home]:
        mine = mine + one.astype(F32)
    grads = mine.astype(LOW)
    return grad_queries, grads[:, :width], grads[:, width:]


def solution(mesh):
    rows = P(("outer", "inner"), None)
    body = functools.partial(shards, mesh.shape["inner"], mesh.shape["outer"])
    return jax.shard_map(
        body, mesh=mesh, in_specs=(rows, rows, rows, rows, P()), out_specs=(rows, rows, rows), check_vma=False
    )
```

```python
import functools
import math

import jax
import jax.numpy as jnp
from jax import lax
from jax.experimental import pallas as pl
from jax.experimental.pallas import tpu as pltpu
from jax.sharding import PartitionSpec as P

BLOCKED = -1e30
F32 = jnp.float32
LOW = jnp.bfloat16


def strides(span):
    return list(range(2, span // 2, 2))


def far_strides(span):
    ways = strides(span)
    return ways[-1:] + ways[:-1]


def window_ids(at, span):
    def nearest(t, u):
        return jnp.where(u < t, u, u - span)

    def same_core(t):
        near = [nearest(t, t ^ d) for d in strides(span)]
        return near, [(t ^ d) - span // 2 for d in far_strides(span)]

    near, far = same_core(at)
    twin = at ^ 1
    twin_near, twin_far = same_core(twin)
    return [at, at - span // 2] + near, far + [nearest(at, twin), twin - span // 2] + twin_near, twin_far


def pack_kernel(k_hbm, v_hbm, kv_ref, arrived):
    width = k_hbm.shape[1]
    copies = [
        pltpu.make_async_copy(one, kv_ref.at[:, pl.ds(i * width, width)], arrived.at[i])
        for i, one in enumerate((k_hbm, v_hbm))
    ]
    for copy in copies:
        copy.start()
    for copy in copies:
        copy.wait()


def group_passes(width, block_len, qt_ref, gt_ref, kv_ref, bias_ref, first, p_ref, dp_ref, sums_ref, top_ref, vt_ref, s_ref):
    pair = 2 * block_len
    slots = kv_ref.shape[0] // block_len
    vt_ref[:width, :] = kv_ref[:, width:].T
    vt_ref[width:, :] = jnp.ones((vt_ref.shape[0] - width, vt_ref.shape[1]), LOW)
    key_pos = lax.broadcasted_iota(jnp.int32, (block_len, pair), 0)
    row_pos = lax.broadcasted_iota(jnp.int32, (block_len, pair), 1) % block_len
    causal = key_pos <= row_pos
    scale2 = width**-0.5 * math.log2(math.e)

    def score(hp):
        lanes = slice(hp * pair, (hp + 1) * pair)
        s = jnp.dot(kv_ref[:, :width], qt_ref[:, lanes], preferred_element_type=F32)
        dp_ref[:, lanes] = jnp.dot(kv_ref[:, width:], gt_ref[:, lanes], preferred_element_type=F32)
        top = None
        for i in range(slots):
            slot = slice(i * block_len, (i + 1) * block_len)
            part = jnp.where(causal, s[slot], BLOCKED) if first + i == 0 else s[slot]
            s_ref[hp % 2, slot, :] = part
            best = jnp.max(part.reshape(-1, 8, pair), axis=0) + bias_ref[8 * (first + i) : 8 * (first + i) + 8, :]
            top = best if top is None else jnp.maximum(top, best)
        top_ref[:, lanes] = jnp.broadcast_to(jnp.max(top, axis=0, keepdims=True) * scale2, (8, pair))

    def weigh(hp):
        lanes = slice(hp * pair, (hp + 1) * pair)
        top = top_ref[0:1, lanes]
        for i in range(slots):
            slot = slice(i * block_len, (i + 1) * block_len)
            shift = bias_ref[8 * (first + i) : 8 * (first + i) + 1, :] - top
            p_ref[slot, lanes] = jnp.exp2(s_ref[hp % 2, slot, :] * scale2 + shift).astype(LOW)
        sums_ref[:, lanes] = jnp.dot(vt_ref[...], p_ref[:, lanes], preferred_element_type=F32)

    return score, weigh


def early_kernel(span, width, block_len, doc_hbm, at_ref, q_hbm, g_hbm, kv_ref, qt_ref, gt_ref, bias_ref, p_ref, dp_ref, sums_ref, top_ref, q_ref, g_ref, doc_ref, arrived, vt_ref, s_ref):
    places = enumerate(((q_hbm, q_ref), (g_hbm, g_ref), (doc_hbm, doc_ref)))
    copies = [pltpu.make_async_copy(there, here, arrived.at[i]) for i, (there, here) in places]
    for copy in copies:
        copy.start()
    pair = 2 * block_len
    score, weigh = group_passes(
        width, block_len, qt_ref, gt_ref, kv_ref, bias_ref, 0, p_ref, dp_ref, sums_ref, top_ref, vt_ref, s_ref
    )
    for copy in copies:
        copy.wait()
    at = at_ref[0]
    own_doc = doc_ref[at]
    for i, one in enumerate(sum(window_ids(at, span), [])):
        allowed = (one >= 0) & (doc_ref[jnp.maximum(one, 0)] == own_doc)
        bias_ref[8 * i : 8 * i + 8, :] = jnp.full((8, pair), jnp.where(allowed, 0.0, BLOCKED).astype(F32))
    pairs = q_ref.shape[1] // width // 2
    for hp in range(-1, pairs):
        if hp + 1 < pairs:
            for h in (2 * hp + 2, 2 * hp + 3):
                qt_ref[:, h * block_len : (h + 1) * block_len] = q_ref[:, h * width : (h + 1) * width].T
                gt_ref[:, h * block_len : (h + 1) * block_len] = g_ref[:, h * width : (h + 1) * width].T
            score(hp + 1)
        if hp >= 0:
            weigh(hp)


def middle_kernel(first, width, block_len, bias_ref, qt_ref, gt_ref, kv_ref, p_ref, dp_ref, sums_ref, top_ref, vt_ref, s_ref):
    score, weigh = group_passes(
        width, block_len, qt_ref, gt_ref, kv_ref, bias_ref, first, p_ref, dp_ref, sums_ref, top_ref, vt_ref, s_ref
    )
    pairs = qt_ref.shape[1] // block_len // 2
    for hp in range(-1, pairs):
        if hp + 1 < pairs:
            score(hp + 1)
        if hp >= 0:
            weigh(hp)


def main_kernel(span, width, block_len, *refs):
    bias_ref, qt_ref, gt_ref, kv_ref = refs[:4]
    early, middle = refs[4:8], refs[8:12]
    first_ref, twin_near_ref, twin_far_ref = refs[12:15]
    ds_refs, sq_refs, sg_refs, factor_refs = refs[15:18], refs[18:20], refs[20:22], refs[22:25]
    late, (vt_ref, s_ref, dk_ref, dv_ref) = refs[25:29], refs[29:]
    scale = width**-0.5
    pairs = qt_ref.shape[1] // block_len // 2
    pair = 2 * block_len
    steps = len(strides(span))
    groups = (early, middle, late)
    score, weigh = group_passes(
        width, block_len, qt_ref, gt_ref, kv_ref, bias_ref, span - steps, *late, vt_ref, s_ref
    )
    nt = (((1,), (1,)), ((), ()))
    twins = ((0, 0), (steps, steps + 2), (0, steps))
    homes = [(first_ref, 0), (twin_far_ref, steps)]
    homes += [(twin_near_ref, i) for i in range(steps)] + [(twin_far_ref, i) for i in range(steps)]
    state = {}

    def rows_of(first, count):
        return slice(first * block_len, (first + count) * block_len)

    def settle(hp):
        lanes = slice(hp * pair, (hp + 1) * pair)
        tops = [top_ref[0:1, lanes] for _, _, _, top_ref in groups]
        top = functools.reduce(jnp.maximum, tops)
        shares = [jnp.exp2(one - top) for one in tops]
        sums = None
        for share, (_, _, sums_ref, _) in zip(shares, groups):
            part = sums_ref[:, lanes] * share
            sums = part if sums is None else sums + part
        inverse = 1.0 / sums[width : width + 1]
        wide_q, wide_g = qt_ref[:, lanes].astype(F32), gt_ref[:, lanes].astype(F32)
        delta = jnp.sum(sums[:width] * wide_g, axis=0, keepdims=True) * inverse
        scaled = []
        for i, share in enumerate(shares):
            factor = inverse * share
            factor_refs[i][:, lanes] = jnp.broadcast_to(factor * scale, (8, pair))
            scaled.append(((wide_q * (factor * scale)).astype(LOW), (wide_g * factor).astype(LOW)))
            if i < 2:
                sq_refs[i][:, lanes], sg_refs[i][:, lanes] = scaled[i]
        state[hp] = (delta, scaled)

    def spread(hp):
        lanes = slice(hp * pair, (hp + 1) * pair)
        delta, scaled = state[hp]
        place = 0
        for (p_ref, dp_ref, _, _), ds_ref, (sq, sg), (first, count) in zip(groups, ds_refs, scaled, twins):
            ds_ref[:, lanes] = (p_ref[:, lanes].astype(F32) * (dp_ref[:, lanes] - delta)).astype(LOW)
            if not count:
                continue
            rows, kept = rows_of(first, count), rows_of(place, count)
            dv = lax.dot_general(p_ref[rows, lanes], sg, nt, preferred_element_type=F32)
            dk = lax.dot_general(ds_ref[rows, lanes], sq, nt, preferred_element_type=F32)
            if hp > 0:
                dk = dk_ref[kept, :] + dk
                dv = dv_ref[kept, :] + dv
            if hp < pairs - 1:
                dk_ref[kept, :] = dk
                dv_ref[kept, :] = dv
            else:
                dk, dv = dk.astype(LOW), dv.astype(LOW)
                for i in range(count):
                    home, where = homes[place + i]
                    home[rows_of(where, 1), :width] = dk[rows_of(i, 1)]
                    home[rows_of(where, 1), width:] = dv[rows_of(i, 1)]
            place += count

    for hp in range(-2, pairs):
        if hp + 2 < pairs:
            score(hp + 2)
        if 0 <= hp + 1 < pairs:
            weigh(hp + 1)
            settle(hp + 1)
        if hp >= 0:
            spread(hp)


def kept_kernel(width, *refs):
    nt = (((1,), (1,)), ((), ()))
    for p_ref, ds_ref, sq_ref, sg_ref, outs in (refs[:4] + (refs[8:11],), refs[4:8] + (refs[11:],)):
        count = sum(ref.shape[0] for ref in outs)
        dk = lax.dot_general(ds_ref[:count, :], sq_ref[...], nt, preferred_element_type=F32).astype(LOW)
        dv = lax.dot_general(p_ref[:count, :], sg_ref[...], nt, preferred_element_type=F32).astype(LOW)
        first = 0
        for ref in outs:
            ref[:, :width] = dk[first : first + ref.shape[0]]
            ref[:, width:] = dv[first : first + ref.shape[0]]
            first += ref.shape[0]


def query_kernel(width, block_len, unused_ref, *refs):
    ds_refs, factor_refs, kv_refs, dq_ref = refs[:3], refs[3:6], refs[6:9], refs[9]
    turned = [kv_ref[:, :width].T for kv_ref in kv_refs]
    pair = 2 * block_len
    for hp in range(dq_ref.shape[1] // width // 2):
        lanes = slice(hp * pair, (hp + 1) * pair)
        dq = None
        for keys, ds_ref, factor_ref in zip(turned, ds_refs, factor_refs):
            part = jnp.dot(keys, ds_ref[:, lanes], preferred_element_type=F32) * factor_ref[0:1, lanes]
            dq = part if dq is None else dq + part
        for h in range(2):
            head = slice((2 * hp + h) * width, (2 * hp + h + 1) * width)
            dq_ref[:, head] = dq[:, h * block_len : (h + 1) * block_len].T.astype(LOW)


HBM = pl.BlockSpec(memory_space=pltpu.HBM)
VMEM = pl.BlockSpec(memory_space=pltpu.VMEM)
SMEM = pl.BlockSpec(memory_space=pltpu.SMEM)


def in_hbm(x):
    return pltpu.with_memory_space_constraint(x, pltpu.HBM)


def call(body, name, ins, outs, scratch, flops, *operands):
    return pl.pallas_call(
        body,
        out_shape=tuple(jax.ShapeDtypeStruct(shape, kind) for shape, kind in outs),
        in_specs=ins,
        out_specs=(VMEM,) * len(outs),
        scratch_shapes=scratch,
        compiler_params=pltpu.CompilerParams(vmem_limit_bytes=24 * 1024 * 1024),
        cost_estimate=pl.CostEstimate(flops=flops, bytes_accessed=1 << 16, transcendentals=0),
        name=name,
    )(*operands)


def shards(inner_count, outer_count, queries, key_rows, value_rows, grad_output, doc_blocks):
    width = key_rows.shape[1]
    block_len = key_rows.shape[0]
    span = inner_count
    half = span // 2
    devices = inner_count * outer_count
    inner_at = lax.axis_index("inner")
    outer_at = lax.axis_index("outer")
    at = outer_at * inner_count + inner_at
    ways, far_ways = strides(span), far_strides(span)

    def place(t):
        return (t % inner_count) * outer_count + t // inner_count

    def moved(x, distance):
        route = [(place(t), place((t + distance) % devices)) for t in range(devices)]
        return lax.ppermute(x, ("inner", "outer"), route)

    def grouped(x, distance):
        return lax.ppermute(x, "outer", [(i, (i + distance) % outer_count) for i in range(outer_count)])

    def returned(x, d):
        route = []
        for t in range(devices):
            u = t ^ d
            route.append((place(t), place(u if u < t else (u - inner_count) % devices)))
        return lax.ppermute(x, ("inner", "outer"), route)

    def swapped(x, d):
        return lax.ppermute(x, "inner", [(i, i ^ d) for i in range(inner_count)])

    def above(d):
        return inner_at > (inner_at ^ d)

    def block(x, i):
        return x[i * block_len : (i + 1) * block_len]

    (own,) = call(
        pack_kernel,
        "pack",
        [HBM, HBM],
        [((block_len, 2 * width), LOW)],
        [pltpu.SemaphoreType.DMA((2,))],
        0,
        *(in_hbm(key_rows), in_hbm(value_rows)),
    )
    prior = grouped(own, 1)
    far = moved(own, half)
    nears = [swapped(jnp.where(above(d), prior, own), d) for d in ways]
    fars = [swapped(far, d) for d in far_ways[:-1]]
    nears[1], later_far = lax.optimization_barrier((nears[1], far))
    nears = jnp.concatenate(nears, axis=0)
    fars.append(swapped(later_far, far_ways[-1]))
    early = jnp.concatenate([own, far, nears], axis=0)
    for_twin = jnp.concatenate([jnp.where(above(1), prior, own), far, nears], axis=0)

    steps = len(ways)
    heads = queries.shape[1] // width
    rows = heads * block_len
    pair = 2 * block_len
    work = 2 * rows * width * block_len
    turned = ((width, rows), LOW)

    def parts(n):
        return ((n * block_len, 2 * width), LOW)

    def sums_of(kv):
        keys = kv.shape[0]
        return [((keys, rows), LOW), ((keys, rows), F32), ((width + 16, rows), F32), ((8, rows), F32)]

    def scratch_of(kv):
        return [pltpu.VMEM((width + 16, kv.shape[0]), LOW), pltpu.VMEM((2, kv.shape[0], pair), F32)]

    qt, gt, bias, *early_sums = call(
        functools.partial(early_kernel, span, width, block_len),
        "early",
        [HBM, SMEM, HBM, HBM, VMEM],
        [turned, turned, ((8 * span, pair), F32)] + sums_of(early),
        [
            pltpu.VMEM(queries.shape, LOW),
            pltpu.VMEM(queries.shape, LOW),
            pltpu.SMEM(doc_blocks.shape, jnp.int32),
            pltpu.SemaphoreType.DMA((3,)),
            *scratch_of(early),
        ],
        40 * work * (steps + 2),
        *(in_hbm(doc_blocks), at.reshape(1), in_hbm(queries), in_hbm(grad_output), early),
    )
    *fars, early_sums[-1] = lax.optimization_barrier((*fars, early_sums[-1]))
    fars = jnp.concatenate(fars, axis=0)
    from_twin, late = swapped(for_twin, 1), swapped(fars, 1)
    middle = jnp.concatenate([fars, from_twin], axis=0)
    middle_sums = call(
        functools.partial(middle_kernel, steps + 2, width, block_len),
        "middle",
        [VMEM] * 4,
        sums_of(middle),
        scratch_of(middle),
        40 * work * (2 * steps + 2),
        *(bias, qt, gt, middle),
    )
    groups = (early, middle, late)
    first_part, twin_near, twin_far, *rest = call(
        functools.partial(main_kernel, span, width, block_len),
        "main",
        [VMEM] * 12,
        [
            *(parts(1), parts(steps), parts(steps + 1)),
            *(((kv.shape[0], rows), LOW) for kv in groups),
            *([turned] * 4),
            *([((8, rows), F32)] * 3),
        ],
        [
            *(pltpu.VMEM(shape, kind) for shape, kind in sums_of(late)),
            *scratch_of(late),
            pltpu.VMEM((span // 2 * block_len, width), F32),
            pltpu.VMEM((span // 2 * block_len, width), F32),
        ],
        6 * work * span,
        *(bias, qt, gt, late, *early_sums, *middle_sums),
    )
    ds, scaled_q, scaled_g, factors = rest[:3], rest[3:5], rest[5:7], rest[7:]
    own_part, far_part, near_parts, far_parts = call(
        functools.partial(kept_kernel, width),
        "kept",
        [VMEM] * 8,
        [parts(1), parts(1), parts(steps), parts(steps)],
        [],
        work * span,
        *(early_sums[0], ds[0], scaled_q[0], scaled_g[0], middle_sums[0], ds[1], scaled_q[1], scaled_g[1]),
    )

    def added(x, y):
        return (x.astype(F32) + y.astype(F32)).astype(LOW)

    from_twin_far = swapped(twin_far, 1)
    from_twin_near = swapped(twin_near, 1)
    far_sums = [added(block(far_parts, i), block(from_twin_far, i)) for i in range(steps)]
    far_back = [swapped(far_sums[far_ways.index(d)], d) for d in reversed(ways)]
    near_sums = [added(block(near_parts, i), block(from_twin_near, i)) for i in range(steps)]
    far_sum = far_part.astype(F32) + block(from_twin_far, steps).astype(F32)
    for one in far_back:
        far_sum = far_sum + one.astype(F32)
    far_sum = far_sum.astype(LOW)
    near_home = [returned(near_sums[ways.index(d)], d) for d in reversed(ways)]
    far_sum, first_part = lax.optimization_barrier((far_sum, first_part))
    far_home = moved(far_sum, -half)
    first_home = returned(first_part, 1)
    (grad_queries,) = call(
        functools.partial(query_kernel, width, block_len),
        "query",
        [pl.BlockSpec(memory_space=pl.ANY)] + [VMEM] * 9,
        [(queries.shape, LOW)],
        [],
        work * span,
        *(first_part, *ds, *factors, *groups),
    )
    mine = own_part.astype(F32)
    for one in near_home + [first_home, far_home]:
        mine = mine + one.astype(F32)
    grads = mine.astype(LOW)
    return grad_queries, grads[:, :width], grads[:, width:]


def solution(mesh):
    rows = P(("outer", "inner"), None)
    body = functools.partial(shards, mesh.shape["inner"], mesh.shape["outer"])
    return jax.shard_map(
        body, mesh=mesh, in_specs=(rows, rows, rows, rows, P()), out_specs=(rows, rows, rows), check_vma=False
    )
```
